512 devices in a mesh: tok: 256 (over z, y, x), head: 2 (over core).
Axes of the slice: x: 4, y: 8, z: 8, core: 2. Of those that a mesh axis runs over, the one named last changes fastest.
Arguments:
- queries: bfloat16 [32768, 1536], P('tok', 'head'), may hold values from -32 to 32
- keys: bfloat16 [32768, 1536], P('tok', 'head'), may hold values from -32 to 32
- values: bfloat16 [32768, 1536], P('tok', 'head'), may hold values from -6 to 6
- window: int32 [256, 27], P('tok'), may hold values from -1 to 255, as said below
- out_weight: bfloat16 [1536, 3072], P('head', 'tok'), may hold values from -0.15625 to 0.15625
Outputs:
- projected: bfloat16 [32768, 3072], P('tok', 'head')
The draws below stay inside these ranges and needn't reach their ends.
Inputs may be any that keep to these rules, and one draw needn't show every extreme that they name: `window`: row i lists distinct tiles: first i itself, then tiles whose frame, row and column each differ from those of i by at most one; -1 marks unused entries, which come last.
All inputs are finite; a program needn't handle non-finite values.
Results may differ from the reference program's by a relative error of at most 0.015.
Values may be sent and summed in bfloat16 or wider, within the bound.
No kernel may reach another device: no remote copies, remote signals or barrier semaphores. Data moves between devices by JAX's collectives and lax.ppermute only.
A program may use at most 128 MiB of HBM per device.

```python
import jax
import jax.numpy as jnp
from jax import lax

D = 3072
HD = 128
HEAD_DEV = 6
TILE = 128
HEADS = 12
HH = 1536
TILES = 256
TW = 8
TH = 4
TF = 8
TOKENS = 32768
N_HEAD = 2


def draw_queries(key, part):
    key = jax.random.fold_in(key, 11)
    drawn = jax.random.normal(key, (TOKENS, HEADS * HD), jnp.float32)
    return drawn.astype(jnp.bfloat16)


def draw_keys(key, part):
    key = jax.random.fold_in(key, 12)
    drawn = jax.random.normal(key, (TOKENS, HEADS * HD), jnp.float32)
    return drawn.astype(jnp.bfloat16)


def draw_window(key, part):
    key = jax.random.fold_in(key, 5)
    frame_size = TW * TH
    tile_index = jnp.arange(TILES, dtype=jnp.int32)[:, None]
    column = jnp.arange(27, dtype=jnp.int32)[None, :]
    step_f = column // 9 - 1
    step_h = column // 3 % 3 - 1
    step_w = column % 3 - 1
    tile_frame = tile_index // frame_size
    tile_row = tile_index // TW % TH
    tile_col = tile_index % TW
    usable = (tile_frame + step_f >= 0) & (tile_frame + step_f < TF) & (tile_row + step_h >= 0) & (tile_row + step_h < TH) & (tile_col + step_w >= 0) & (tile_col + step_w < TW) & (column != 13)
    candidate = tile_index + step_f * frame_size + step_h * TW + step_w
    row_keys = jax.random.split(jax.random.fold_in(key, 1), TILES)
    shuffled = jax.vmap(lambda row_key: jax.random.permutation(row_key, 27))(row_keys).astype(jnp.int32)
    ranking = jnp.where(usable, shuffled, shuffled + 1000)
    order = jnp.argsort(ranking, axis=1)
    ordered = jnp.take_along_axis(candidate, order, axis=1)
    available = jnp.sum(usable.astype(jnp.int32), axis=1)
    wanted = jax.random.randint(jax.random.fold_in(key, 2), (TILES,), 8, 27)
    wanted = jnp.where(tile_index[:, 0] % 5 == 0, 26, wanted)
    listed_count = jnp.minimum(wanted, available)
    others = jnp.where(column < listed_count[:, None], ordered, -1)
    return jnp.concatenate([tile_index, others[:, :26]], axis=1).astype(jnp.int32)


def levels(rng, extent, cuts, smallest, largest):
    def one(position, blocks):
        heights = jax.random.uniform(jax.random.fold_in(jax.random.fold_in(rng, 6), position), (blocks,), jnp.float32, smallest / len(cuts), largest / len(cuts))
        return jnp.repeat(jnp.exp(heights), extent[position] // blocks).reshape((-1,) + (1,) * (len(extent) - position - 1))

    factor_of = one(*cuts[0])
    for cut in cuts[1:]:
        factor_of = factor_of * one(*cut)
    return factor_of


def scatter_about(rng, extent, spread, most, cuts=(), kind=jnp.bfloat16):
    array = spread * jax.random.normal(rng, extent, jnp.float32)
    if cuts:
        array = array * levels(rng, extent, cuts, -0.22, 0.18)
    return jnp.clip(array, -most, most).astype(kind)


def setup_inputs(seed: int = 0) -> dict:
    key_list = jax.random.split(jax.random.key(seed), 6)
    queries = draw_queries(jax.random.fold_in(key_list[5], 71), 0)
    keys = draw_keys(jax.random.fold_in(key_list[5], 71), 0)
    values = scatter_about(key_list[2], (TOKENS, HH), 1.0, 6.0, ((0, 256), (1, 2)))
    window = draw_window(jax.random.fold_in(key_list[5], 71), 0)
    out_weight = scatter_about(key_list[4], (HH, D), HH ** -0.5, 0.15625, ((0, 2), (1, 256)))
    return {"queries": queries, "keys": keys, "values": values, "window": window, "out_weight": out_weight}


def reference(queries, keys, values, window, out_weight):
    scale = HD ** -0.5
    query_tiles = queries.reshape(TILES, TILE, HEADS, HD)
    key_tiles = keys.reshape(TILES, TILE, HEADS, HD)
    value_tiles = values.reshape(TILES, TILE, HEADS, HD)

    def per_tile(tile_index):
        listed_tiles = window[tile_index]
        is_listed = listed_tiles >= 0
        safe_index = jnp.where(is_listed, listed_tiles, 0).astype(jnp.int32)
        chosen_keys = key_tiles[safe_index].astype(jnp.float32)
        chosen_values = value_tiles[safe_index].astype(jnp.float32)
        query_block = query_tiles[tile_index].astype(jnp.float32)
        scores = jnp.einsum("qhd,wkhd->hqwk", query_block, chosen_keys) * scale
        scores = jnp.where(is_listed[None, None, :, None], scores, -jnp.inf)
        peak = jnp.max(scores, axis=(2, 3), keepdims=True)
        unrounded = jnp.exp(scores - peak)
        total = jnp.sum(unrounded, axis=(2, 3))
        weights = lax.optimization_barrier(unrounded.astype(jnp.bfloat16)).astype(jnp.float32)
        summed = jnp.einsum("hqwk,wkhd->qhd", weights, chosen_values)
        return (summed / jnp.transpose(total)[:, :, None]).astype(jnp.bfloat16)

    attended = lax.map(per_tile, jnp.arange(TILES, dtype=jnp.int32)).reshape(TOKENS, HEADS * HD)
    group_width = HEAD_DEV * HD
    projected = jnp.zeros((TOKENS, D), jnp.float32)
    for head_group in range(N_HEAD):
        lower = head_group * group_width
        partial_sum = jnp.dot(attended[:, lower:lower + group_width], out_weight[lower:lower + group_width],
                              preferred_element_type=jnp.float32)
        projected = projected + lax.optimization_barrier(partial_sum.astype(jnp.bfloat16)).astype(jnp.float32)
    return projected.astype(jnp.bfloat16)
```

```python
import functools

import jax
import jax.numpy as jnp
import numpy as np
from jax import lax
from jax.experimental import pallas as pl
from jax.experimental.pallas import tpu as pltpu
from jax.sharding import Mesh, PartitionSpec as P

HD = 128
TILE = 128
HEADS = 6
FEAT = HEADS * HD
TF, TH, TW = 8, 4, 8
TILES = TF * TH * TW
ALL = ("z", "y", "x", "head")
TOK = ("z", "y", "x")
FACTOR = float(HD**-0.5 * np.log2(np.e))
OFFSETS = (0, 1, -1)
FLAG_ROWS = 16


def place(tile):
    return tile // (TH * TW), tile // TW % TH, tile % TW


def from_neighbour(offset_of_core):
    pairs = []
    for tile in range(TILES):
        for core in range(2):
            f, r, c = (a + b for a, b in zip(place(tile), offset_of_core(core)))
            if 0 <= f < TF and 0 <= r < TH and 0 <= c < TW:
                source = (f * TH + r) * TW + c
                pairs.append((2 * source + core, 2 * tile + core))
    return pairs


def first_axis(step):
    return from_neighbour(lambda core: (step, 0, 0) if core == 0 else (0, 0, step))


def second_axis(step):
    return from_neighbour(lambda core: (0, 0, step) if core == 0 else (step, 0, 0))


def row_axis(step):
    return from_neighbour(lambda core: (0, step, 0))


def biases(window, my_tile, core):
    slot = jnp.arange(27, dtype=jnp.int32)

    def step(digit):
        return jnp.where(digit == 2, -1, digit)

    dr, da, db = step(slot // 9), step(slot // 3 % 3), step(slot % 3)
    df = jnp.where(core == 0, da, db)
    dc = jnp.where(core == 0, db, da)
    f, r, c = place(my_tile)
    inside = (
        (f + df >= 0) & (f + df < TF) & (r + dr >= 0) & (r + dr < TH) & (c + dc >= 0) & (c + dc < TW)
    )
    tile = my_tile + (df * TH + dr) * TW + dc
    listed = inside & jnp.any(window[0][None, :] == tile[:, None], axis=1)
    return jnp.where(listed, 0.0, -1e30).astype(jnp.bfloat16).reshape(3, 9)


def with_biases(queries, bias):
    rows = jnp.zeros((FLAG_ROWS,), jnp.bfloat16).at[:9].set(bias)
    return jnp.concatenate([queries, jnp.broadcast_to(rows[:, None], (FLAG_ROWS, queries.shape[1]))])


def attention_kernel(q0, qp, qm, kv, ap, am, bp, bm, o0, s0, op, om):
    q_refs = (q0, qp, qm)
    bias = []
    for ref in q_refs:
        rows = ref[TILE : TILE + FLAG_ROWS, :HD].astype(jnp.float32)
        bias.append([rows[j : j + 1, :] for j in range(9)])
    tiles = []
    for a, ref in enumerate((kv, ap, am)):
        tiles.append((ref, 0))
        tiles.append((bp, 2 * TILE * a))
        tiles.append((bm, 2 * TILE * a))
    lane = lax.broadcasted_iota(jnp.int32, (TILE, HD), 1)

    def head(h, stats):
        cols = pl.ds(pl.multiple_of(h * HD, HD), HD)
        k = jnp.concatenate([ref[pl.ds(lo, TILE), cols] for ref, lo in tiles], axis=0)
        v = jnp.concatenate([ref[pl.ds(lo + TILE, TILE), cols] for ref, lo in tiles], axis=0)
        new_stats = []
        for i, ref in enumerate(q_refs):
            scores = lax.dot_general(
                ref[pl.ds(0, TILE), cols], k, (((1,), (1,)), ((), ())), preferred_element_type=jnp.float32
            )
            shifted = jnp.concatenate(
                [scores[:, j * TILE : (j + 1) * TILE] * FACTOR + bias[i][j] for j in range(9)], axis=1
            )
            peak = jnp.max(shifted, axis=1, keepdims=True).astype(jnp.bfloat16).astype(jnp.float32)
            unrounded = jnp.exp2(shifted - peak)
            total = jnp.sum(unrounded, axis=1, keepdims=True)
            summed = jnp.dot(unrounded.astype(jnp.bfloat16), v, preferred_element_type=jnp.float32)
            if i == 0:
                o0[:, cols] = summed
                high = total
                low = jnp.zeros_like(total)
            else:
                (op, om)[i - 1][:, cols] = summed.astype(jnp.bfloat16)
                high = total.astype(jnp.bfloat16).astype(jnp.float32)
                low = total - high
            s = jnp.where(lane == h, peak, stats[i])
            s = jnp.where(lane == h + 8, high, s)
            s = jnp.where(lane == h + 16, low, s)
            new_stats.append(s)
        return tuple(new_stats)

    zero = jnp.zeros((TILE, HD), jnp.float32)
    stats = lax.fori_loop(0, HEADS, head, (zero, zero, zero))
    s0[...] = stats[0]
    op[:, FEAT:] = stats[1].astype(jnp.bfloat16)
    om[:, FEAT:] = stats[2].astype(jnp.bfloat16)


def attention(*operands):
    vmem = pl.BlockSpec(memory_space=pltpu.VMEM)
    back = jax.ShapeDtypeStruct((TILE, FEAT + HD), jnp.bfloat16)
    return pl.pallas_call(
        attention_kernel,
        out_shape=(
            jax.ShapeDtypeStruct((TILE, FEAT), jnp.float32),
            jax.ShapeDtypeStruct((TILE, HD), jnp.float32),
            back,
            back,
        ),
        in_specs=[vmem] * len(operands),
        out_specs=(vmem,) * 4,
        compiler_params=pltpu.CompilerParams(vmem_limit_bytes=40 * 1024 * 1024),
        cost_estimate=pl.CostEstimate(
            flops=4 * 27 * TILE * TILE * FEAT, bytes_accessed=6 * 2**20, transcendentals=27 * TILE * TILE * HEADS
        ),
    )(*operands)


def merge_kernel(o0, s0, op, om, out):
    for h in range(HEADS):
        cols = slice(h * HD, (h + 1) * HD)
        peaks, totals, sums = [s0[:, h : h + 1]], [s0[:, h + 8 : h + 9]], [o0[:, cols]]
        for ref in (op, om):
            stats = ref[:, FEAT:].astype(jnp.float32)
            total = stats[:, h + 8 : h + 9] + stats[:, h + 16 : h + 17]
            peaks.append(jnp.where(total > 0, stats[:, h : h + 1], -1e30))
            totals.append(total)
            sums.append(ref[:, cols].astype(jnp.float32))
        peak = jnp.maximum(jnp.maximum(peaks[0], peaks[1]), peaks[2])
        factors = [jnp.exp2(p - peak) for p in peaks]
        total = sum(f * t for f, t in zip(factors, totals))
        summed = sum(f * s for f, s in zip(factors, sums))
        out[:, cols] = (summed / total).astype(jnp.bfloat16)


def merge(*operands):
    vmem = pl.BlockSpec(memory_space=pltpu.VMEM)
    return pl.pallas_call(
        merge_kernel,
        out_shape=jax.ShapeDtypeStruct((TILE, FEAT), jnp.bfloat16),
        in_specs=[vmem] * len(operands),
        out_specs=vmem,
        cost_estimate=pl.CostEstimate(flops=10 * TILE * FEAT, bytes_accessed=2**20, transcendentals=0),
    )(*operands)


def body(queries, keys, values, window, out_weight):
    my_tile = lax.axis_index(TOK)
    core = lax.axis_index("head")
    kv = jnp.concatenate([keys, values])
    ap = lax.ppermute(kv, ALL, first_axis(1))
    am = lax.ppermute(kv, ALL, first_axis(-1))
    weight = lax.all_gather(out_weight.T, TOK)
    bias = biases(window, my_tile, core)
    q0 = with_biases(queries, bias[0])
    qp = lax.ppermute(with_biases(queries, bias[2]), ALL, row_axis(1))
    qm = lax.ppermute(with_biases(queries, bias[1]), ALL, row_axis(-1))
    line = jnp.concatenate([kv, ap, am])
    bp = lax.ppermute(line, ALL, second_axis(1))
    bm = lax.ppermute(line, ALL, second_axis(-1))
    o0, s0, op, om = attention(q0, qp, qm, kv, ap, am, bp, bm)
    back_p = lax.ppermute(om, ALL, row_axis(1))
    back_m = lax.ppermute(op, ALL, row_axis(-1))
    attended = merge(o0, s0, back_p, back_m)
    partial = lax.dot_general(
        attended, weight.reshape(-1, FEAT), (((1,), (1,)), ((), ())), preferred_element_type=jnp.float32
    )
    half = partial.shape[1] // 2
    mine = lax.dynamic_slice_in_dim(partial, core * half, half, 1)
    other = lax.dynamic_slice_in_dim(partial, (1 - core) * half, half, 1).astype(jnp.bfloat16)
    received = lax.ppermute(other, "head", [(0, 1), (1, 0)])
    return (mine + received.astype(jnp.float32)).astype(jnp.bfloat16)


def solution(mesh):
    fine = Mesh(mesh.devices.reshape(8, 8, 4, 2), ALL)
    in_specs = (P(TOK, "head"), P(TOK, "head"), P(TOK, "head"), P(TOK, None), P("head", TOK))
    return jax.shard_map(body, mesh=fine, in_specs=in_specs, out_specs=P(TOK, "head"), check_vma=False)
```

```python
import functools

import jax
import jax.numpy as jnp
import numpy as np
from jax import lax
from jax.experimental import pallas as pl
from jax.experimental.pallas import tpu as pltpu
from jax.sharding import Mesh, PartitionSpec as P

HD = 128
TILE = 128
HEADS = 6
FEAT = HEADS * HD
TF, TH, TW = 8, 4, 8
TILES = TF * TH * TW
ALL = ("z", "y", "x", "head")
TOK = ("z", "y", "x")
FACTOR = float(HD**-0.5 * np.log2(np.e))
OFFSETS = (0, 1, -1)
FLAG_ROWS = 16


def place(tile):
    return tile // (TH * TW), tile // TW % TH, tile % TW


def from_neighbour(offset_of_core):
    pairs = []
    for tile in range(TILES):
        for core in range(2):
            f, r, c = (a + b for a, b in zip(place(tile), offset_of_core(core)))
            if 0 <= f < TF and 0 <= r < TH and 0 <= c < TW:
                source = (f * TH + r) * TW + c
                pairs.append((2 * source + core, 2 * tile + core))
    return pairs


def first_axis(step):
    return from_neighbour(lambda core: (step, 0, 0) if core == 0 else (0, 0, step))


def second_axis(step):
    return from_neighbour(lambda core: (0, 0, step) if core == 0 else (step, 0, 0))


def row_axis(step):
    return from_neighbour(lambda core: (0, step, 0))


def biases(window, my_tile, core):
    slot = jnp.arange(27, dtype=jnp.int32)

    def step(digit):
        return jnp.where(digit == 2, -1, digit)

    dr, da, db = step(slot // 9), step(slot // 3 % 3), step(slot % 3)
    df = jnp.where(core == 0, da, db)
    dc = jnp.where(core == 0, db, da)
    f, r, c = place(my_tile)
    inside = (
        (f + df >= 0) & (f + df < TF) & (r + dr >= 0) & (r + dr < TH) & (c + dc >= 0) & (c + dc < TW)
    )
    tile = my_tile + (df * TH + dr) * TW + dc
    listed = inside & jnp.any(window[0][None, :] == tile[:, None], axis=1)
    return jnp.where(listed, 0.0, -1e30).astype(jnp.bfloat16).reshape(3, 9)


def with_biases(queries, bias):
    rows = jnp.zeros((FLAG_ROWS,), jnp.bfloat16).at[:9].set(bias)
    return jnp.concatenate([queries, jnp.broadcast_to(rows[:, None], (FLAG_ROWS, queries.shape[1]))])


def attention_kernel(groups, query_count, with_state, message, *refs):
    refs = list(refs)
    q_refs = [refs.pop(0) for _ in range(query_count)]
    kv_refs = [refs.pop(0) for _ in range(max(g[0] for g in groups) + 1)]
    old_sum, old_stats = (refs.pop(0), refs.pop(0)) if with_state else (None, None)
    rows = query_count * TILE
    bias = []
    for ref in q_refs:
        block = ref[TILE : TILE + FLAG_ROWS, :HD].astype(jnp.float32)
        bias.append([block[j : j + 1, :] for _, _, j in groups])
    lane = lax.broadcasted_iota(jnp.int32, (rows, HD), 1)
    stats = jnp.zeros((rows, HD), jnp.float32)
    for h in range(HEADS):
        cols = slice(h * HD, (h + 1) * HD)
        q = jnp.concatenate([ref[:TILE, cols] for ref in q_refs], axis=0)
        k = jnp.concatenate([kv_refs[n][lo : lo + TILE, cols] for n, lo, _ in groups], axis=0)
        v = jnp.concatenate([kv_refs[n][lo + TILE : lo + 2 * TILE, cols] for n, lo, _ in groups], axis=0)
        scores = lax.dot_general(q, k, (((1,), (1,)), ((), ())), preferred_element_type=jnp.float32)
        shifted = jnp.concatenate(
            [
                jnp.concatenate(
                    [
                        scores[i * TILE : (i + 1) * TILE, j * TILE : (j + 1) * TILE] * FACTOR + bias[i][j]
                        for j in range(len(groups))
                    ],
                    axis=1,
                )
                for i in range(query_count)
            ],
            axis=0,
        )
        peak = jnp.max(shifted, axis=1, keepdims=True)
        if with_state:
            old_peak = old_stats[:, h : h + 1]
            peak = jnp.maximum(peak, old_peak)
        peak = peak.astype(jnp.bfloat16).astype(jnp.float32)
        unrounded = jnp.exp2(shifted - peak)
        total = jnp.sum(unrounded, axis=1, keepdims=True)
        summed = jnp.dot(unrounded.astype(jnp.bfloat16), v, preferred_element_type=jnp.float32)
        if with_state:
            factor = jnp.exp2(old_peak - peak)
            total = total + factor * old_stats[:, h + 8 : h + 9]
            summed = summed + factor * old_sum[:, cols]
        stats = jnp.where(lane == h, peak, stats)
        if message:
            high = total.astype(jnp.bfloat16).astype(jnp.float32)
            stats = jnp.where(lane == h + 8, high, stats)
            stats = jnp.where(lane == h + 16, total - high, stats)
            for i in range(query_count):
                refs[i][:, cols] = summed[i * TILE : (i + 1) * TILE].astype(jnp.bfloat16)
        else:
            stats = jnp.where(lane == h + 8, total, stats)
            refs[0][:, cols] = summed
    if message:
        for i in range(query_count):
            refs[i][:, FEAT:] = stats[i * TILE : (i + 1) * TILE].astype(jnp.bfloat16)
    else:
        refs[1][...] = stats


VMEM = pl.BlockSpec(memory_space=pltpu.VMEM)


def attention(queries, pieces, groups, state=None, message=False):
    count = len(queries)
    rows = count * TILE
    if message:
        out_shape = (jax.ShapeDtypeStruct((TILE, FEAT + HD), jnp.bfloat16),) * count
    else:
        out_shape = (
            jax.ShapeDtypeStruct((rows, FEAT), jnp.float32),
            jax.ShapeDtypeStruct((rows, HD), jnp.float32),
        )
    in_specs = [VMEM] * (count + len(pieces))
    operands = [*queries, *pieces]
    if state is not None:
        (total_rows, which), arrays = state
        for array in arrays:
            in_specs.append(pl.BlockSpec((rows, array.shape[1]), lambda i: (which, 0)))
            operands.append(array)
    pairs = count * len(groups)
    return pl.pallas_call(
        functools.partial(attention_kernel, groups, count, state is not None, message),
        grid=(1,),
        out_shape=out_shape,
        in_specs=in_specs,
        out_specs=(VMEM,) * len(out_shape),
        compiler_params=pltpu.CompilerParams(vmem_limit_bytes=40 * 1024 * 1024),
        cost_estimate=pl.CostEstimate(
            flops=4 * pairs * TILE * TILE * FEAT,
            bytes_accessed=len(groups) * 4 * TILE * FEAT,
            transcendentals=pairs * TILE * TILE * HEADS,
        ),
    )(*operands)


def merge_kernel(o0, s0, op, om, out):
    own = s0[...]
    peaks, totals, sums = [own], [pltpu.roll(own, HD - 8, 1)], [o0]
    for ref in (op, om):
        stats = ref[:, FEAT:].astype(jnp.float32)
        total = pltpu.roll(stats, HD - 8, 1) + pltpu.roll(stats, HD - 16, 1)
        peaks.append(jnp.where(total > 0, stats, -1e30))
        totals.append(total)
        sums.append(ref)
    peak = jnp.maximum(jnp.maximum(peaks[0], peaks[1]), peaks[2])
    factors = [jnp.exp2(p - peak) for p in peaks]
    total = sum(f * t for f, t in zip(factors, totals))
    shares = [f / total for f in factors]
    for h in range(HEADS):
        cols = slice(h * HD, (h + 1) * HD)
        parts = [w[:, h : h + 1] * ref[:, cols].astype(jnp.float32) for w, ref in zip(shares, sums)]
        out[:, cols] = (parts[0] + parts[1] + parts[2]).astype(jnp.bfloat16)


def merge(*operands):
    return pl.pallas_call(
        merge_kernel,
        out_shape=jax.ShapeDtypeStruct((TILE, FEAT), jnp.bfloat16),
        in_specs=[VMEM] * len(operands),
        out_specs=VMEM,
        cost_estimate=pl.CostEstimate(flops=10 * TILE * FEAT, bytes_accessed=2**20, transcendentals=0),
    )(*operands)


def project_kernel(_, rows, weight, out):
    product = lax.dot_general(
        rows[...], weight[...], (((1,), (1,)), ((), ())), preferred_element_type=jnp.float32
    )
    out[...] = product.astype(out.dtype)


def project(rows, weight, which, dtype):
    half = weight.shape[0] // 2
    return pl.pallas_call(
        project_kernel,
        grid_spec=pltpu.PrefetchScalarGridSpec(
            num_scalar_prefetch=1,
            grid=(1,),
            in_specs=[
                pl.BlockSpec(rows.shape, lambda i, c: (0, 0)),
                pl.BlockSpec((half, FEAT), lambda i, c: (c[0], 0)),
            ],
            out_specs=pl.BlockSpec((rows.shape[0], half), lambda i, c: (0, 0)),
        ),
        out_shape=jax.ShapeDtypeStruct((rows.shape[0], half), dtype),
        compiler_params=pltpu.CompilerParams(vmem_limit_bytes=40 * 1024 * 1024),
        cost_estimate=pl.CostEstimate(
            flops=2 * rows.shape[0] * half * FEAT, bytes_accessed=3 * 2**20, transcendentals=0
        ),
    )(which[None], rows, weight)


PAD = 16
SHARE = 12
WIDE = 8 * 4 * SHARE


def column_order():
    order = np.zeros((4, 8, PAD, WIDE), np.float32)
    for x in range(4):
        for p in range(8):
            y = (p & 1) * 4 + (p & 2) + (p >> 2)
            for j in range(SHARE):
                order[x, p, j, (y * 4 + x) * SHARE + j] = 1
    return order.reshape(4 * HD, WIDE)


def arrange_kernel(pieces, order, out):
    for z in range(4):
        block = jnp.concatenate([pieces[x, :, z * HD : (z + 1) * HD] for x in range(4)], axis=1)
        product = jnp.dot(block, order[...], preferred_element_type=jnp.float32)
        out[:, z * WIDE : (z + 1) * WIDE] = product.astype(jnp.bfloat16)


def arrange(pieces):
    return pl.pallas_call(
        arrange_kernel,
        out_shape=jax.ShapeDtypeStruct((TILE, 4 * WIDE), jnp.bfloat16),
        in_specs=[VMEM, VMEM],
        out_specs=VMEM,
        cost_estimate=pl.CostEstimate(flops=2 * TILE * 4 * HD * 4 * WIDE, bytes_accessed=2**20, transcendentals=0),
    )(pieces, jnp.asarray(column_order(), jnp.bfloat16))


def gathered_weight(out_weight):
    part = jnp.pad(out_weight.T, ((0, PAD - SHARE), (0, 0)))
    y = lax.axis_index("y")
    for bit in (4, 2, 1):
        other = lax.ppermute(part, "y", [(i, i ^ bit) for i in range(8)])
        upper = (y & bit) != 0
        part = jnp.concatenate([jnp.where(upper, other, part), jnp.where(upper, part, other)])
    return part


def body(queries, keys, values, window, out_weight):
    my_tile = lax.axis_index(TOK)
    core = lax.axis_index("head")
    kv = jnp.concatenate([keys, values])
    ap = lax.ppermute(kv, ALL, first_axis(1))
    am = lax.ppermute(kv, ALL, first_axis(-1))
    weight = lax.all_gather(gathered_weight(out_weight), "z", tiled=True)
    bias = biases(window, my_tile, core)
    q0 = with_biases(queries, bias[0])
    qp = lax.ppermute(with_biases(queries, bias[2]), ALL, row_axis(1))
    qm = lax.ppermute(with_biases(queries, bias[1]), ALL, row_axis(-1))
    line = jnp.concatenate([kv, ap, am])
    bp = lax.ppermute(line, ALL, second_axis(1))
    bm = lax.ppermute(line, ALL, second_axis(-1))
    near = [(n, 0, 3 * n) for n in range(3)]
    far = [(n, 2 * TILE * a, 3 * a + n + 1) for n in range(2) for a in range(3)]
    state = attention((qp, qm, q0), (kv, ap, am), near)
    op, om = attention((qp, qm), (bp, bm), far, ((3, 0), state), message=True)
    back_p = lax.ppermute(om, ALL, row_axis(1))
    back_m = lax.ppermute(op, ALL, row_axis(-1))
    o0, s0 = attention((q0,), (bp, bm), far, ((3, 2), state))
    attended = merge(o0, s0, back_p, back_m)
    rows = lax.all_gather(attended, "x", tiled=True)
    other = project(rows, weight, 1 - core, jnp.bfloat16)
    received = lax.ppermute(other, "head", [(0, 1), (1, 0)])
    mine = project(rows, weight, core, jnp.float32)
    columns = (mine + received.astype(jnp.float32)).astype(jnp.bfloat16)
    pieces = lax.all_to_all(columns.reshape(4, TILE, -1), "x", 0, 0)
    return arrange(pieces)


def solution(mesh):
    fine = Mesh(mesh.devices.reshape(8, 8, 4, 2), ALL)
    in_specs = (P(TOK, "head"), P(TOK, "head"), P(TOK, "head"), P(TOK, None), P("head", TOK))
    return jax.shard_map(body, mesh=fine, in_specs=in_specs, out_specs=P(TOK, "head"), check_vma=False)
```

```python
import functools

import jax
import jax.numpy as jnp
import numpy as np
from jax import lax
from jax.experimental import pallas as pl
from jax.experimental.pallas import tpu as pltpu
from jax.sharding import Mesh, PartitionSpec as P

HD = 128
TILE = 128
HEADS = 6
FEAT = HEADS * HD
TF, TH, TW = 8, 4, 8
TILES = TF * TH * TW
ALL = ("z", "y", "x", "head")
TOK = ("z", "y", "x")
FACTOR = float(HD**-0.5 * np.log2(np.e))
OFFSETS = (0, 1, -1)
FLAG_ROWS = 16


def place(tile):
    return tile // (TH * TW), tile // TW % TH, tile % TW


def from_neighbour(offset_of_core):
    pairs = []
    for tile in range(TILES):
        for core in range(2):
            f, r, c = (a + b for a, b in zip(place(tile), offset_of_core(core)))
            if 0 <= f < TF and 0 <= r < TH and 0 <= c < TW:
                source = (f * TH + r) * TW + c
                pairs.append((2 * source + core, 2 * tile + core))
    return pairs


def first_axis(step):
    return from_neighbour(lambda core: (step, 0, 0) if core == 0 else (0, 0, step))


def second_axis(step):
    return from_neighbour(lambda core: (0, 0, step) if core == 0 else (step, 0, 0))


def row_axis(step):
    return from_neighbour(lambda core: (0, step, 0))


def biases(window, my_tile, core):
    slot = jnp.arange(27, dtype=jnp.int32)

    def step(digit):
        return jnp.where(digit == 2, -1, digit)

    dr, da, db = step(slot // 9), step(slot // 3 % 3), step(slot % 3)
    df = jnp.where(core == 0, da, db)
    dc = jnp.where(core == 0, db, da)
    f, r, c = place(my_tile)
    inside = (
        (f + df >= 0) & (f + df < TF) & (r + dr >= 0) & (r + dr < TH) & (c + dc >= 0) & (c + dc < TW)
    )
    tile = my_tile + (df * TH + dr) * TW + dc
    listed = inside & jnp.any(window[0][None, :] == tile[:, None], axis=1)
    return jnp.where(listed, 0.0, -1e30).astype(jnp.bfloat16).reshape(3, 9)


def with_biases(queries, bias):
    rows = jnp.zeros((FLAG_ROWS,), jnp.bfloat16).at[:9].set(bias)
    return jnp.concatenate([queries, jnp.broadcast_to(rows[:, None], (FLAG_ROWS, queries.shape[1]))])


def attention_kernel(groups, query_count, with_state, message, *refs):
    refs = list(refs)
    q_refs = [refs.pop(0) for _ in range(query_count)]
    kv_refs = [refs.pop(0) for _ in range(max(g[0] for g in groups) + 1)]
    old_sum, old_stats = (refs.pop(0), refs.pop(0)) if with_state else (None, None)
    rows = query_count * TILE
    bias = []
    for ref in q_refs:
        block = ref[TILE : TILE + FLAG_ROWS, :HD].astype(jnp.float32)
        bias.append([block[j : j + 1, :] for _, _, j in groups])
    lane = lax.broadcasted_iota(jnp.int32, (rows, HD), 1)
    stats = jnp.zeros((rows, HD), jnp.float32)
    for h in range(HEADS):
        cols = slice(h * HD, (h + 1) * HD)
        q = jnp.concatenate([ref[:TILE, cols] for ref in q_refs], axis=0)
        k = jnp.concatenate([kv_refs[n][lo : lo + TILE, cols] for n, lo, _ in groups], axis=0)
        v = jnp.concatenate([kv_refs[n][lo + TILE : lo + 2 * TILE, cols] for n, lo, _ in groups], axis=0)
        scores = lax.dot_general(q, k, (((1,), (1,)), ((), ())), preferred_element_type=jnp.float32)
        shifted = jnp.concatenate(
            [
                jnp.concatenate(
                    [
                        scores[i * TILE : (i + 1) * TILE, j * TILE : (j + 1) * TILE] * FACTOR + bias[i][j]
                        for j in range(len(groups))
                    ],
                    axis=1,
                )
                for i in range(query_count)
            ],
            axis=0,
        )
        peak = jnp.max(shifted, axis=1, keepdims=True)
        if with_state:
            old_peak = old_stats[:, h : h + 1]
            peak = jnp.maximum(peak, old_peak)
        peak = peak.astype(jnp.bfloat16).astype(jnp.float32)
        unrounded = jnp.exp2(shifted - peak)
        total = jnp.sum(unrounded, axis=1, keepdims=True)
        summed = jnp.dot(unrounded.astype(jnp.bfloat16), v, preferred_element_type=jnp.float32)
        if with_state:
            factor = jnp.exp2(old_peak - peak)
            total = total + factor * old_stats[:, h + 8 : h + 9]
            summed = summed + factor * old_sum[:, cols]
        stats = jnp.where(lane == h, peak, stats)
        if message:
            high = total.astype(jnp.bfloat16).astype(jnp.float32)
            stats = jnp.where(lane == h + 8, high, stats)
            stats = jnp.where(lane == h + 16, total - high, stats)
            for i in range(query_count):
                refs[i][:, cols] = summed[i * TILE : (i + 1) * TILE].astype(jnp.bfloat16)
        else:
            stats = jnp.where(lane == h + 8, total, stats)
            refs[0][:, cols] = summed
    if message:
        for i in range(query_count):
            refs[i][:, FEAT:] = stats[i * TILE : (i + 1) * TILE].astype(jnp.bfloat16)
    else:
        refs[1][...] = stats


VMEM = pl.BlockSpec(memory_space=pltpu.VMEM)


def attention(queries, pieces, groups, state=None, message=False):
    count = len(queries)
    rows = count * TILE
    if message:
        out_shape = (jax.ShapeDtypeStruct((TILE, FEAT + HD), jnp.bfloat16),) * count
    else:
        out_shape = (
            jax.ShapeDtypeStruct((rows, FEAT), jnp.float32),
            jax.ShapeDtypeStruct((rows, HD), jnp.float32),
        )
    in_specs = [VMEM] * (count + len(pieces))
    operands = [*queries, *pieces]
    if state is not None:
        (total_rows, which), arrays = state
        for array in arrays:
            in_specs.append(pl.BlockSpec((rows, array.shape[1]), lambda i: (which, 0)))
            operands.append(array)
    pairs = count * len(groups)
    return pl.pallas_call(
        functools.partial(attention_kernel, groups, count, state is not None, message),
        grid=(1,),
        out_shape=out_shape,
        in_specs=in_specs,
        out_specs=(VMEM,) * len(out_shape),
        compiler_params=pltpu.CompilerParams(vmem_limit_bytes=12 * 1024 * 1024),
        cost_estimate=pl.CostEstimate(
            flops=160 * pairs * TILE * TILE * FEAT,
            bytes_accessed=len(groups) * 4 * TILE * FEAT,
            transcendentals=pairs * TILE * TILE * HEADS,
        ),
    )(*operands)


def merge_kernel(o0, s0, op, om, out):
    own = s0[...]
    peaks, totals, sums = [own], [pltpu.roll(own, HD - 8, 1)], [o0]
    for ref in (op, om):
        stats = ref[:, FEAT:].astype(jnp.float32)
        total = pltpu.roll(stats, HD - 8, 1) + pltpu.roll(stats, HD - 16, 1)
        peaks.append(jnp.where(total > 0, stats, -1e30))
        totals.append(total)
        sums.append(ref)
    peak = jnp.maximum(jnp.maximum(peaks[0], peaks[1]), peaks[2])
    factors = [jnp.exp2(p - peak) for p in peaks]
    total = sum(f * t for f, t in zip(factors, totals))
    shares = [f / total for f in factors]
    for h in range(HEADS):
        cols = slice(h * HD, (h + 1) * HD)
        parts = [w[:, h : h + 1] * ref[:, cols].astype(jnp.float32) for w, ref in zip(shares, sums)]
        out[:, cols] = (parts[0] + parts[1] + parts[2]).astype(jnp.bfloat16)


def merge(*operands):
    return pl.pallas_call(
        merge_kernel,
        out_shape=jax.ShapeDtypeStruct((TILE, FEAT), jnp.bfloat16),
        in_specs=[VMEM] * len(operands),
        out_specs=VMEM,
        compiler_params=pltpu.CompilerParams(vmem_limit_bytes=12 * 1024 * 1024),
        cost_estimate=pl.CostEstimate(flops=10 * TILE * FEAT, bytes_accessed=2**20, transcendentals=0),
    )(*operands)


def project_kernel(_, rows, weight, out):
    product = lax.dot_general(
        rows[...], weight[...], (((1,), (1,)), ((), ())), preferred_element_type=jnp.float32
    )
    out[...] = product.astype(out.dtype)


def project(rows, weight, which, dtype):
    half = weight.shape[0] // 2
    return pl.pallas_call(
        project_kernel,
        grid_spec=pltpu.PrefetchScalarGridSpec(
            num_scalar_prefetch=1,
            grid=(1,),
            in_specs=[
                pl.BlockSpec(rows.shape, lambda i, c: (0, 0)),
                pl.BlockSpec((half, FEAT), lambda i, c: (c[0], 0)),
            ],
            out_specs=pl.BlockSpec((rows.shape[0], half), lambda i, c: (0, 0)),
        ),
        out_shape=jax.ShapeDtypeStruct((rows.shape[0], half), dtype),
        compiler_params=pltpu.CompilerParams(vmem_limit_bytes=12 * 1024 * 1024),
        cost_estimate=pl.CostEstimate(
            flops=2 * rows.shape[0] * half * FEAT, bytes_accessed=3 * 2**20, transcendentals=0
        ),
    )(which[None], rows, weight)


PAD = 16
SHARE = 12
WIDE = 8 * 4 * SHARE


def column_order():
    order = np.zeros((4, 8, PAD, WIDE), np.float32)
    for x in range(4):
        for p in range(8):
            y = (p & 1) * 4 + (p & 2) + (p >> 2)
            for j in range(SHARE):
                order[x, p, j, (y * 4 + x) * SHARE + j] = 1
    return order.reshape(4 * HD, WIDE)


def arrange_kernel(pieces, order, out):
    for z in range(4):
        block = jnp.concatenate([pieces[x, :, z * HD : (z + 1) * HD] for x in range(4)], axis=1)
        product = jnp.dot(block, order[...], preferred_element_type=jnp.float32)
        out[:, z * WIDE : (z + 1) * WIDE] = product.astype(jnp.bfloat16)


def arrange(pieces):
    return pl.pallas_call(
        arrange_kernel,
        out_shape=jax.ShapeDtypeStruct((TILE, 4 * WIDE), jnp.bfloat16),
        in_specs=[VMEM, VMEM],
        out_specs=VMEM,
        compiler_params=pltpu.CompilerParams(vmem_limit_bytes=12 * 1024 * 1024),
        cost_estimate=pl.CostEstimate(flops=2 * TILE * 4 * HD * 4 * WIDE, bytes_accessed=2**20, transcendentals=0),
    )(pieces, jnp.asarray(column_order(), jnp.bfloat16))


def gathered_weight(part, bits):
    y = lax.axis_index("y")
    for bit in bits:
        other = lax.ppermute(part, "y", [(i, i ^ bit) for i in range(8)])
        upper = (y & bit) != 0
        part = jnp.concatenate([jnp.where(upper, other, part), jnp.where(upper, part, other)])
    return part


def body(queries, keys, values, window, out_weight):
    my_tile = lax.axis_index(TOK)
    core = lax.axis_index("head")
    kv = jnp.concatenate([keys, values])
    ap = lax.ppermute(kv, ALL, first_axis(1))
    am = lax.ppermute(kv, ALL, first_axis(-1))
    part = gathered_weight(jnp.pad(out_weight.T, ((0, PAD - SHARE), (0, 0))), (4,))
    bias = biases(window, my_tile, core)
    q0 = with_biases(queries, bias[0])
    qp = lax.ppermute(with_biases(queries, bias[2]), ALL, row_axis(1))
    qm = lax.ppermute(with_biases(queries, bias[1]), ALL, row_axis(-1))
    ap, am, qp, qm, part = lax.optimization_barrier((ap, am, qp, qm, part))
    line = jnp.concatenate([kv, ap, am])
    weight = lax.all_gather(gathered_weight(part, (2, 1)), "z", tiled=True)
    bp = lax.ppermute(line, ALL, second_axis(1))
    bm = lax.ppermute(line, ALL, second_axis(-1))
    near = [(n, 0, 3 * n) for n in range(3)]
    far = [(n, 2 * TILE * a, 3 * a + n + 1) for n in range(2) for a in range(3)]
    state = attention((qp, qm, q0), (kv, ap, am), near)
    op, om = attention((qp, qm), (bp, bm), far, ((3, 0), state), message=True)
    back_p = lax.ppermute(om, ALL, row_axis(1))
    back_m = lax.ppermute(op, ALL, row_axis(-1))
    o0, s0 = attention((q0,), (bp, bm), far, ((3, 2), state))
    attended = merge(o0, s0, back_p, back_m)
    rows = lax.all_gather(attended, "x", tiled=True)
    other = project(rows, weight, 1 - core, jnp.bfloat16)
    received = lax.ppermute(other, "head", [(0, 1), (1, 0)])
    mine = project(rows, weight, core, jnp.float32)
    columns = (mine + received.astype(jnp.float32)).astype(jnp.bfloat16)
    pieces = lax.all_to_all(columns.reshape(4, TILE, -1), "x", 0, 0)
    return arrange(pieces)


def solution(mesh):
    fine = Mesh(mesh.devices.reshape(8, 8, 4, 2), ALL)
    in_specs = (P(TOK, "head"), P(TOK, "head"), P(TOK, "head"), P(TOK, None), P("head", TOK))
    return jax.shard_map(body, mesh=fine, in_specs=in_specs, out_specs=P(TOK, "head"), check_vma=False)
```

```python
import functools

import jax
import jax.numpy as jnp
import numpy as np
from jax import lax
from jax.experimental import pallas as pl
from jax.experimental.pallas import tpu as pltpu
from jax.sharding import Mesh, PartitionSpec as P

HD = 128
TILE = 128
HEADS = 6
FEAT = HEADS * HD
TF, TH, TW = 8, 4, 8
TILES = TF * TH * TW
ALL = ("z", "y", "x", "head")
TOK = ("z", "y", "x")
FACTOR = float(HD**-0.5 * np.log2(np.e))
OFFSETS = (0, 1, -1)
FLAG_ROWS = 16


def place(tile):
    return tile // (TH * TW), tile // TW % TH, tile % TW


def from_neighbour(offset_of_core):
    pairs = []
    for tile in range(TILES):
        for core in range(2):
            f, r, c = (a + b for a, b in zip(place(tile), offset_of_core(core)))
            if 0 <= f < TF and 0 <= r < TH and 0 <= c < TW:
                source = (f * TH + r) * TW + c
                pairs.append((2 * source + core, 2 * tile + core))
    return pairs


def first_axis(step):
    return from_neighbour(lambda core: (step, 0, 0) if core == 0 else (0, 0, step))


def second_axis(step):
    return from_neighbour(lambda core: (0, 0, step) if core == 0 else (step, 0, 0))


def row_axis(step):
    return from_neighbour(lambda core: (0, step, 0))


def biases(window, my_tile, core):
    slot = jnp.arange(27, dtype=jnp.int32)

    def step(digit):
        return jnp.where(digit == 2, -1, digit)

    dr, da, db = step(slot // 9), step(slot // 3 % 3), step(slot % 3)
    df = jnp.where(core == 0, da, db)
    dc = jnp.where(core == 0, db, da)
    f, r, c = place(my_tile)
    inside = (
        (f + df >= 0) & (f + df < TF) & (r + dr >= 0) & (r + dr < TH) & (c + dc >= 0) & (c + dc < TW)
    )
    tile = my_tile + (df * TH + dr) * TW + dc
    listed = inside & jnp.any(window[0][None, :] == tile[:, None], axis=1)
    return jnp.where(listed, 0.0, -1e30).astype(jnp.bfloat16).reshape(3, 9)


def with_biases(queries, bias):
    rows = jnp.zeros((FLAG_ROWS,), jnp.bfloat16).at[:9].set(bias)
    return jnp.concatenate([queries, jnp.broadcast_to(rows[:, None], (FLAG_ROWS, queries.shape[1]))])


def attention_kernel(groups, query_count, with_state, message, *refs):
    refs = list(refs)
    q_refs = [refs.pop(0) for _ in range(query_count)]
    kv_refs = [refs.pop(0) for _ in range(max(g[0] for g in groups) + 1)]
    old_sum, old_stats = (refs.pop(0), refs.pop(0)) if with_state else (None, None)
    rows = query_count * TILE
    bias = []
    for ref in q_refs:
        block = ref[TILE : TILE + FLAG_ROWS, :HD].astype(jnp.float32)
        bias.append([block[j : j + 1, :] for _, _, j in groups])
    lane = lax.broadcasted_iota(jnp.int32, (rows, HD), 1)
    stats = jnp.zeros((rows, HD), jnp.float32)
    for h in range(HEADS):
        cols = slice(h * HD, (h + 1) * HD)
        q = jnp.concatenate([ref[:TILE, cols] for ref in q_refs], axis=0)
        k = jnp.concatenate([kv_refs[n][lo : lo + TILE, cols] for n, lo, _ in groups], axis=0)
        v = jnp.concatenate([kv_refs[n][lo + TILE : lo + 2 * TILE, cols] for n, lo, _ in groups], axis=0)
        scores = lax.dot_general(q, k, (((1,), (1,)), ((), ())), preferred_element_type=jnp.float32)
        shifted = jnp.concatenate(
            [
                jnp.concatenate(
                    [
                        scores[i * TILE : (i + 1) * TILE, j * TILE : (j + 1) * TILE] * FACTOR + bias[i][j]
                        for j in range(len(groups))
                    ],
                    axis=1,
                )
                for i in range(query_count)
            ],
            axis=0,
        )
        peak = jnp.max(shifted, axis=1, keepdims=True)
        if with_state:
            old_peak = old_stats[:, h : h + 1]
            peak = jnp.maximum(peak, old_peak)
        peak = peak.astype(jnp.bfloat16).astype(jnp.float32)
        unrounded = jnp.exp2(shifted - peak)
        total = jnp.sum(unrounded, axis=1, keepdims=True)
        summed = jnp.dot(unrounded.astype(jnp.bfloat16), v, preferred_element_type=jnp.float32)
        if with_state:
            factor = jnp.exp2(old_peak - peak)
            total = total + factor * old_stats[:, h + 8 : h + 9]
            summed = summed + factor * old_sum[:, cols]
        stats = jnp.where(lane == h, peak, stats)
        if message:
            high = total.astype(jnp.bfloat16).astype(jnp.float32)
            stats = jnp.where(lane == h + 8, high, stats)
            stats = jnp.where(lane == h + 16, total - high, stats)
            for i in range(query_count):
                refs[i][:, cols] = summed[i * TILE : (i + 1) * TILE].astype(jnp.bfloat16)
        else:
            stats = jnp.where(lane == h + 8, total, stats)
            refs[0][:, cols] = summed
    if message:
        for i in range(query_count):
            refs[i][:, FEAT:] = stats[i * TILE : (i + 1) * TILE].astype(jnp.bfloat16)
    else:
        refs[1][...] = stats


VMEM = pl.BlockSpec(memory_space=pltpu.VMEM)


def attention(queries, pieces, groups, state=None, message=False):
    count = len(queries)
    rows = count * TILE
    if message:
        out_shape = (jax.ShapeDtypeStruct((TILE, FEAT + HD), jnp.bfloat16),) * count
    else:
        out_shape = (
            jax.ShapeDtypeStruct((rows, FEAT), jnp.float32),
            jax.ShapeDtypeStruct((rows, HD), jnp.float32),
        )
    in_specs = [VMEM] * (count + len(pieces))
    operands = [*queries, *pieces]
    if state is not None:
        (total_rows, which), arrays = state
        for array in arrays:
            in_specs.append(pl.BlockSpec((rows, array.shape[1]), lambda i: (which, 0)))
            operands.append(array)
    pairs = count * len(groups)
    return pl.pallas_call(
        functools.partial(attention_kernel, groups, count, state is not None, message),
        grid=(1,),
        out_shape=out_shape,
        in_specs=in_specs,
        out_specs=(VMEM,) * len(out_shape),
        compiler_params=pltpu.CompilerParams(vmem_limit_bytes=12 * 1024 * 1024),
        cost_estimate=pl.CostEstimate(
            flops=160 * pairs * TILE * TILE * FEAT,
            bytes_accessed=len(groups) * 4 * TILE * FEAT,
            transcendentals=pairs * TILE * TILE * HEADS,
        ),
    )(*operands)


def merge_kernel(o0, s0, op, om, out):
    own = s0[...]
    peaks, totals, sums = [own], [pltpu.roll(own, HD - 8, 1)], [o0]
    for ref in (op, om):
        stats = ref[:, FEAT:].astype(jnp.float32)
        total = pltpu.roll(stats, HD - 8, 1) + pltpu.roll(stats, HD - 16, 1)
        peaks.append(jnp.where(total > 0, stats, -1e30))
        totals.append(total)
        sums.append(ref)
    peak = jnp.maximum(jnp.maximum(peaks[0], peaks[1]), peaks[2])
    factors = [jnp.exp2(p - peak) for p in peaks]
    total = sum(f * t for f, t in zip(factors, totals))
    shares = [f / total for f in factors]
    for h in range(HEADS):
        cols = slice(h * HD, (h + 1) * HD)
        parts = [w[:, h : h + 1] * ref[:, cols].astype(jnp.float32) for w, ref in zip(shares, sums)]
        out[:, cols] = (parts[0] + parts[1] + parts[2]).astype(jnp.bfloat16)


def merge(*operands):
    return pl.pallas_call(
        merge_kernel,
        out_shape=jax.ShapeDtypeStruct((TILE, FEAT), jnp.bfloat16),
        in_specs=[VMEM] * len(operands),
        out_specs=VMEM,
        compiler_params=pltpu.CompilerParams(vmem_limit_bytes=12 * 1024 * 1024),
        cost_estimate=pl.CostEstimate(flops=10 * TILE * FEAT, bytes_accessed=2**20, transcendentals=0),
    )(*operands)


def project_kernel(_, rows, weight, out):
    product = lax.dot_general(
        rows[...], weight[...], (((1,), (1,)), ((), ())), preferred_element_type=jnp.float32
    )
    out[...] = product.astype(out.dtype)


def project(rows, weight, which, dtype):
    half = weight.shape[0] // 2
    return pl.pallas_call(
        project_kernel,
        grid_spec=pltpu.PrefetchScalarGridSpec(
            num_scalar_prefetch=1,
            grid=(1,),
            in_specs=[
                pl.BlockSpec(rows.shape, lambda i, c: (0, 0)),
                pl.BlockSpec((half, FEAT), lambda i, c: (c[0], 0)),
            ],
            out_specs=pl.BlockSpec((rows.shape[0], half), lambda i, c: (0, 0)),
        ),
        out_shape=jax.ShapeDtypeStruct((rows.shape[0], half), dtype),
        compiler_params=pltpu.CompilerParams(vmem_limit_bytes=12 * 1024 * 1024),
        cost_estimate=pl.CostEstimate(
            flops=2 * rows.shape[0] * half * FEAT, bytes_accessed=3 * 2**20, transcendentals=0
        ),
    )(which[None], rows, weight)


PAD = 16
SHARE = 12
WIDE = 8 * 4 * SHARE


def column_order():
    order = np.zeros((4, 8, PAD, WIDE), np.float32)
    for x in range(4):
        for p in range(8):
            for j in range(SHARE):
                order[x, p, j, (p * 4 + x) * SHARE + j] = 1
    return order.reshape(4 * HD, WIDE)


def arrange_kernel(pieces, order, out):
    for z in range(4):
        block = jnp.concatenate([pieces[x, :, z * HD : (z + 1) * HD] for x in range(4)], axis=1)
        product = jnp.dot(block, order[...], preferred_element_type=jnp.float32)
        out[:, z * WIDE : (z + 1) * WIDE] = product.astype(jnp.bfloat16)


def arrange(pieces):
    return pl.pallas_call(
        arrange_kernel,
        out_shape=jax.ShapeDtypeStruct((TILE, 4 * WIDE), jnp.bfloat16),
        in_specs=[VMEM, VMEM],
        out_specs=VMEM,
        compiler_params=pltpu.CompilerParams(vmem_limit_bytes=12 * 1024 * 1024),
        cost_estimate=pl.CostEstimate(flops=2 * TILE * 4 * HD * 4 * WIDE, bytes_accessed=2**20, transcendentals=0),
    )(pieces, jnp.asarray(column_order(), jnp.bfloat16))


def body(queries, keys, values, window, out_weight):
    my_tile = lax.axis_index(TOK)
    core = lax.axis_index("head")
    kv = jnp.concatenate([keys, values])
    ap = lax.ppermute(kv, ALL, first_axis(1))
    am = lax.ppermute(kv, ALL, first_axis(-1))
    part = jnp.pad(out_weight.T, ((0, PAD - SHARE), (0, 0)))
    weight = lax.all_to_all(jnp.broadcast_to(part, (64, PAD, FEAT)), ("z", "y"), 0, 0).reshape(-1, FEAT)
    bias = biases(window, my_tile, core)
    q0 = with_biases(queries, bias[0])
    qp = lax.ppermute(with_biases(queries, bias[2]), ALL, row_axis(1))
    qm = lax.ppermute(with_biases(queries, bias[1]), ALL, row_axis(-1))
    ap, am, qp, qm = lax.optimization_barrier((ap, am, qp, qm))
    line = jnp.concatenate([kv, ap, am])
    bp = lax.ppermute(line, ALL, second_axis(1))
    bm = lax.ppermute(line, ALL, second_axis(-1))
    near = [(n, 0, 3 * n) for n in range(3)]
    far = [(n, 2 * TILE * a, 3 * a + n + 1) for n in range(2) for a in range(3)]
    state = attention((qp, qm, q0), (kv, ap, am), near)
    op, om = attention((qp, qm), (bp, bm), far, ((3, 0), state), message=True)
    back_p = lax.ppermute(om, ALL, row_axis(1))
    back_m = lax.ppermute(op, ALL, row_axis(-1))
    o0, s0 = attention((q0,), (bp, bm), far, ((3, 2), state))
    attended = merge(o0, s0, back_p, back_m)
    rows = lax.all_gather(attended, "x", tiled=True)
    other = project(rows, weight, 1 - core, jnp.bfloat16)
    received = lax.ppermute(other, "head", [(0, 1), (1, 0)])
    mine = project(rows, weight, core, jnp.float32)
    columns = (mine + received.astype(jnp.float32)).astype(jnp.bfloat16)
    pieces = lax.all_to_all(columns.reshape(4, TILE, -1), "x", 0, 0)
    return arrange(pieces)


def solution(mesh):
    fine = Mesh(mesh.devices.reshape(8, 8, 4, 2), ALL)
    in_specs = (P(TOK, "head"), P(TOK, "head"), P(TOK, "head"), P(TOK, None), P("head", TOK))
    return jax.shard_map(body, mesh=fine, in_specs=in_specs, out_specs=P(TOK, "head"), check_vma=False)
```

```python
import functools

import jax
import jax.numpy as jnp
import numpy as np
from jax import lax
from jax.experimental import pallas as pl
from jax.experimental.pallas import tpu as pltpu
from jax.sharding import Mesh, PartitionSpec as P

HD = 128
TILE = 128
HEADS = 6
FEAT = HEADS * HD
TF, TH, TW = 8, 4, 8
TILES = TF * TH * TW
ALL = ("z", "y", "x", "head")
TOK = ("z", "y", "x")
FACTOR = float(HD**-0.5 * np.log2(np.e))
OFFSETS = (0, 1, -1)
FLAG_ROWS = 16


def place(tile):
    return tile // (TH * TW), tile // TW % TH, tile % TW


def from_neighbour(offset_of_core):
    pairs = []
    for tile in range(TILES):
        for core in range(2):
            f, r, c = (a + b for a, b in zip(place(tile), offset_of_core(core)))
            if 0 <= f < TF and 0 <= r < TH and 0 <= c < TW:
                source = (f * TH + r) * TW + c
                pairs.append((2 * source + core, 2 * tile + core))
    return pairs


def first_axis(step):
    return from_neighbour(lambda core: (step, 0, 0) if core == 0 else (0, 0, step))


def second_axis(step):
    return from_neighbour(lambda core: (0, 0, step) if core == 0 else (step, 0, 0))


def row_axis(step):
    return from_neighbour(lambda core: (0, step, 0))


def biases(window, my_tile, core):
    slot = jnp.arange(27, dtype=jnp.int32)

    def step(digit):
        return jnp.where(digit == 2, -1, digit)

    dr, da, db = step(slot // 9), step(slot // 3 % 3), step(slot % 3)
    df = jnp.where(core == 0, da, db)
    dc = jnp.where(core == 0, db, da)
    f, r, c = place(my_tile)
    inside = (
        (f + df >= 0) & (f + df < TF) & (r + dr >= 0) & (r + dr < TH) & (c + dc >= 0) & (c + dc < TW)
    )
    tile = my_tile + (df * TH + dr) * TW + dc
    listed = inside & jnp.any(window[0][None, :] == tile[:, None], axis=1)
    return jnp.where(listed, 0.0, -1e30).astype(jnp.bfloat16).reshape(3, 9)


def with_biases(queries, bias):
    rows = jnp.zeros((FLAG_ROWS,), jnp.bfloat16).at[:9].set(bias)
    return jnp.concatenate([queries, jnp.broadcast_to(rows[:, None], (FLAG_ROWS, queries.shape[1]))])


def attention_kernel(groups, query_count, with_state, message, *refs):
    refs = list(refs)
    q_refs = [refs.pop(0) for _ in range(query_count)]
    kv_refs = [refs.pop(0) for _ in range(max(g[0] for g in groups) + 1)]
    old_sum, old_stats = (refs.pop(0), refs.pop(0)) if with_state else (None, None)
    rows = query_count * TILE
    bias = []
    for ref in q_refs:
        block = ref[TILE : TILE + FLAG_ROWS, :HD].astype(jnp.float32)
        bias.append([block[j : j + 1, :] for _, _, j in groups])
    lane = lax.broadcasted_iota(jnp.int32, (rows, HD), 1)
    stats = jnp.zeros((rows, HD), jnp.float32)
    for h in range(HEADS):
        cols = slice(h * HD, (h + 1) * HD)
        q = jnp.concatenate([ref[:TILE, cols] for ref in q_refs], axis=0)
        k = jnp.concatenate([kv_refs[n][lo : lo + TILE, cols] for n, lo, _ in groups], axis=0)
        v = jnp.concatenate([kv_refs[n][lo + TILE : lo + 2 * TILE, cols] for n, lo, _ in groups], axis=0)
        scores = lax.dot_general(q, k, (((1,), (1,)), ((), ())), preferred_element_type=jnp.float32)
        shifted = jnp.concatenate(
            [
                jnp.concatenate(
                    [
                        scores[i * TILE : (i + 1) * TILE, j * TILE : (j + 1) * TILE] * FACTOR + bias[i][j]
                        for j in range(len(groups))
                    ],
                    axis=1,
                )
                for i in range(query_count)
            ],
            axis=0,
        )
        peak = jnp.max(shifted, axis=1, keepdims=True)
        if with_state:
            old_peak = old_stats[:, h : h + 1]
            peak = jnp.maximum(peak, old_peak)
        peak = peak.astype(jnp.bfloat16).astype(jnp.float32)
        unrounded = jnp.exp2(shifted - peak)
        total = jnp.sum(unrounded, axis=1, keepdims=True)
        summed = jnp.dot(unrounded.astype(jnp.bfloat16), v, preferred_element_type=jnp.float32)
        if with_state:
            factor = jnp.exp2(old_peak - peak)
            total = total + factor * old_stats[:, h + 8 : h + 9]
            summed = summed + factor * old_sum[:, cols]
        stats = jnp.where(lane == h, peak, stats)
        if message:
            high = total.astype(jnp.bfloat16).astype(jnp.float32)
            stats = jnp.where(lane == h + 8, high, stats)
            stats = jnp.where(lane == h + 16, total - high, stats)
            for i in range(query_count):
                refs[i][:, cols] = summed[i * TILE : (i + 1) * TILE].astype(jnp.bfloat16)
        else:
            stats = jnp.where(lane == h + 8, total, stats)
            refs[0][:, cols] = summed
    if message:
        for i in range(query_count):
            refs[i][:, FEAT:] = stats[i * TILE : (i + 1) * TILE].astype(jnp.bfloat16)
    else:
        refs[1][...] = stats


VMEM = pl.BlockSpec(memory_space=pltpu.VMEM)


def attention(queries, pieces, groups, state=None, message=False):
    count = len(queries)
    rows = count * TILE
    if message:
        out_shape = (jax.ShapeDtypeStruct((TILE, FEAT + HD), jnp.bfloat16),) * count
    else:
        out_shape = (
            jax.ShapeDtypeStruct((rows, FEAT), jnp.float32),
            jax.ShapeDtypeStruct((rows, HD), jnp.float32),
        )
    in_specs = [VMEM] * (count + len(pieces))
    operands = [*queries, *pieces]
    if state is not None:
        (total_rows, which), arrays = state
        for array in arrays:
            in_specs.append(pl.BlockSpec((rows, array.shape[1]), lambda i: (which, 0)))
            operands.append(array)
    pairs = count * len(groups)
    return pl.pallas_call(
        functools.partial(attention_kernel, groups, count, state is not None, message),
        grid=(1,),
        out_shape=out_shape,
        in_specs=in_specs,
        out_specs=(VMEM,) * len(out_shape),
        compiler_params=pltpu.CompilerParams(vmem_limit_bytes=12 * 1024 * 1024),
        cost_estimate=pl.CostEstimate(
            flops=160 * pairs * TILE * TILE * FEAT,
            bytes_accessed=len(groups) * 4 * TILE * FEAT,
            transcendentals=pairs * TILE * TILE * HEADS,
        ),
    )(*operands)


def stack_kernel(*refs):
    low = 0
    for ref in refs[:-1]:
        refs[-1][low : low + ref.shape[0], :] = ref[...]
        low += ref.shape[0]


def stacked(*arrays):
    rows = sum(a.shape[0] for a in arrays)
    return pl.pallas_call(
        stack_kernel,
        out_shape=jax.ShapeDtypeStruct((rows, arrays[0].shape[1]), arrays[0].dtype),
        in_specs=[VMEM] * len(arrays),
        out_specs=VMEM,
        compiler_params=pltpu.CompilerParams(vmem_limit_bytes=12 * 1024 * 1024),
        cost_estimate=pl.CostEstimate(flops=0, bytes_accessed=4 * rows * FEAT, transcendentals=0),
    )(*arrays)


def merge_kernel(o0, s0, op, om, out):
    own = s0[...]
    peaks, totals, sums = [own], [pltpu.roll(own, HD - 8, 1)], [o0]
    for ref in (op, om):
        stats = ref[:, FEAT:].astype(jnp.float32)
        total = pltpu.roll(stats, HD - 8, 1) + pltpu.roll(stats, HD - 16, 1)
        peaks.append(jnp.where(total > 0, stats, -1e30))
        totals.append(total)
        sums.append(ref)
    peak = jnp.maximum(jnp.maximum(peaks[0], peaks[1]), peaks[2])
    factors = [jnp.exp2(p - peak) for p in peaks]
    total = sum(f * t for f, t in zip(factors, totals))
    shares = [f / total for f in factors]
    for h in range(HEADS):
        cols = slice(h * HD, (h + 1) * HD)
        parts = [w[:, h : h + 1] * ref[:, cols].astype(jnp.float32) for w, ref in zip(shares, sums)]
        out[:, cols] = (parts[0] + parts[1] + parts[2]).astype(jnp.bfloat16)


def merge(*operands):
    return pl.pallas_call(
        merge_kernel,
        out_shape=jax.ShapeDtypeStruct((TILE, FEAT), jnp.bfloat16),
        in_specs=[VMEM] * len(operands),
        out_specs=VMEM,
        compiler_params=pltpu.CompilerParams(vmem_limit_bytes=12 * 1024 * 1024),
        cost_estimate=pl.CostEstimate(flops=10 * TILE * FEAT, bytes_accessed=2**20, transcendentals=0),
    )(*operands)


def project_kernel(_, rows, weight, out):
    product = lax.dot_general(
        rows[...], weight[...], (((1,), (1,)), ((), ())), preferred_element_type=jnp.float32
    )
    out[...] = product.astype(out.dtype)


def project(rows, weight, which, dtype):
    half = weight.shape[0] // 2
    return pl.pallas_call(
        project_kernel,
        grid_spec=pltpu.PrefetchScalarGridSpec(
            num_scalar_prefetch=1,
            grid=(1,),
            in_specs=[
                pl.BlockSpec(rows.shape, lambda i, c: (0, 0)),
                pl.BlockSpec((half, FEAT), lambda i, c: (c[0], 0)),
            ],
            out_specs=pl.BlockSpec((rows.shape[0], half), lambda i, c: (0, 0)),
        ),
        out_shape=jax.ShapeDtypeStruct((rows.shape[0], half), dtype),
        compiler_params=pltpu.CompilerParams(vmem_limit_bytes=12 * 1024 * 1024),
        cost_estimate=pl.CostEstimate(
            flops=2 * rows.shape[0] * half * FEAT, bytes_accessed=3 * 2**20, transcendentals=0
        ),
    )(which[None], rows, weight)


PAD = 16
SHARE = 12
WIDE = 8 * 4 * SHARE


def column_order():
    order = np.zeros((4, 8, PAD, WIDE), np.float32)
    for x in range(4):
        for p in range(8):
            for j in range(SHARE):
                order[x, p, j, (p * 4 + x) * SHARE + j] = 1
    return order.reshape(4 * HD, WIDE)


def arrange_kernel(pieces, order, out):
    for z in range(4):
        block = jnp.concatenate([pieces[x, :, z * HD : (z + 1) * HD] for x in range(4)], axis=1)
        product = jnp.dot(block, order[...], preferred_element_type=jnp.float32)
        out[:, z * WIDE : (z + 1) * WIDE] = product.astype(jnp.bfloat16)


def arrange(pieces):
    return pl.pallas_call(
        arrange_kernel,
        out_shape=jax.ShapeDtypeStruct((TILE, 4 * WIDE), jnp.bfloat16),
        in_specs=[VMEM, VMEM],
        out_specs=VMEM,
        compiler_params=pltpu.CompilerParams(vmem_limit_bytes=12 * 1024 * 1024),
        cost_estimate=pl.CostEstimate(flops=2 * TILE * 4 * HD * 4 * WIDE, bytes_accessed=2**20, transcendentals=0),
    )(pieces, jnp.asarray(column_order(), jnp.bfloat16))


def body(queries, keys, values, window, out_weight):
    my_tile = lax.axis_index(TOK)
    core = lax.axis_index("head")
    kv = stacked(keys, values)
    ap = lax.ppermute(kv, ALL, first_axis(1))
    am = lax.ppermute(kv, ALL, first_axis(-1))
    part = jnp.pad(out_weight.T, ((0, PAD - SHARE), (0, 0)))
    line_y = lax.all_to_all(jnp.broadcast_to(part, (8, PAD, FEAT)), "y", 0, 0)
    weight = lax.all_gather(line_y.reshape(-1, FEAT), "z", tiled=True)
    bias = biases(window, my_tile, core)
    q0 = with_biases(queries, bias[0])
    qp = lax.ppermute(with_biases(queries, bias[2]), ALL, row_axis(1))
    qm = lax.ppermute(with_biases(queries, bias[1]), ALL, row_axis(-1))
    ap, am, qp, qm = lax.optimization_barrier((ap, am, qp, qm))
    line = stacked(kv, ap, am)
    bp = lax.ppermute(line, ALL, second_axis(1))
    bm = lax.ppermute(line, ALL, second_axis(-1))
    near = [(n, 0, 3 * n) for n in range(3)]
    far = [(n, 2 * TILE * a, 3 * a + n + 1) for n in range(2) for a in range(3)]
    state = attention((qp, qm, q0), (kv, ap, am), near)
    op, om = attention((qp, qm), (bp, bm), far, ((3, 0), state), message=True)
    back_p = lax.ppermute(om, ALL, row_axis(1))
    back_m = lax.ppermute(op, ALL, row_axis(-1))
    o0, s0 = attention((q0,), (bp, bm), far, ((3, 2), state))
    attended = merge(o0, s0, back_p, back_m)
    rows = lax.all_gather(attended, "x", tiled=True)
    other = project(rows, weight, 1 - core, jnp.bfloat16)
    received = lax.ppermute(other, "head", [(0, 1), (1, 0)])
    mine = project(rows, weight, core, jnp.float32)
    columns = (mine + received.astype(jnp.float32)).astype(jnp.bfloat16)
    pieces = lax.all_to_all(columns.reshape(4, TILE, -1), "x", 0, 0)
    return arrange(pieces)


def solution(mesh):
    fine = Mesh(mesh.devices.reshape(8, 8, 4, 2), ALL)
    in_specs = (P(TOK, "head"), P(TOK, "head"), P(TOK, "head"), P(TOK, None), P("head", TOK))
    return jax.shard_map(body, mesh=fine, in_specs=in_specs, out_specs=P(TOK, "head"), check_vma=False)
```

```python
import functools

import jax
import jax.numpy as jnp
import numpy as np
from jax import lax
from jax.experimental import pallas as pl
from jax.experimental.pallas import tpu as pltpu
from jax.sharding import Mesh, PartitionSpec as P

HD = 128
TILE = 128
HEADS = 6
FEAT = HEADS * HD
TF, TH, TW = 8, 4, 8
TILES = TF * TH * TW
ALL = ("z", "y", "x", "head")
TOK = ("z", "y", "x")
FACTOR = float(HD**-0.5 * np.log2(np.e))
OFFSETS = (0, 1, -1)
FLAG_ROWS = 16


def place(tile):
    return tile // (TH * TW), tile // TW % TH, tile % TW


def from_neighbour(offset_of_core):
    pairs = []
    for tile in range(TILES):
        for core in range(2):
            f, r, c = (a + b for a, b in zip(place(tile), offset_of_core(core)))
            if 0 <= f < TF and 0 <= r < TH and 0 <= c < TW:
                source = (f * TH + r) * TW + c
                pairs.append((2 * source + core, 2 * tile + core))
    return pairs


def first_axis(step):
    return from_neighbour(lambda core: (step, 0, 0) if core == 0 else (0, 0, step))


def second_axis(step):
    return from_neighbour(lambda core: (0, 0, step) if core == 0 else (step, 0, 0))


def row_axis(step):
    return from_neighbour(lambda core: (0, step, 0))


def biases(window, my_tile, core):
    slot = jnp.arange(27, dtype=jnp.int32)

    def step(digit):
        return jnp.where(digit == 2, -1, digit)

    dr, da, db = step(slot // 9), step(slot // 3 % 3), step(slot % 3)
    df = jnp.where(core == 0, da, db)
    dc = jnp.where(core == 0, db, da)
    f, r, c = place(my_tile)
    inside = (
        (f + df >= 0) & (f + df < TF) & (r + dr >= 0) & (r + dr < TH) & (c + dc >= 0) & (c + dc < TW)
    )
    tile = my_tile + (df * TH + dr) * TW + dc
    listed = inside & jnp.any(window[0][None, :] == tile[:, None], axis=1)
    return jnp.where(listed, 0.0, -1e30).astype(jnp.bfloat16).reshape(3, 9)


def with_biases(queries, bias):
    rows = jnp.zeros((FLAG_ROWS,), jnp.bfloat16).at[:9].set(bias)
    return jnp.concatenate([queries, jnp.broadcast_to(rows[:, None], (FLAG_ROWS, queries.shape[1]))])


def attention_kernel(groups, query_count, with_state, message, *refs):
    refs = list(refs)
    q_refs = [refs.pop(0) for _ in range(query_count)]
    kv_refs = [refs.pop(0) for _ in range(max(g[0] for g in groups) + 1)]
    old_sum, old_stats = (refs.pop(0), refs.pop(0)) if with_state else (None, None)
    rows = query_count * TILE
    bias = []
    for ref in q_refs:
        block = ref[TILE : TILE + FLAG_ROWS, :HD].astype(jnp.float32)
        bias.append([block[j : j + 1, :] for _, _, j in groups])
    lane = lax.broadcasted_iota(jnp.int32, (rows, HD), 1)
    stats = jnp.zeros((rows, HD), jnp.float32)
    for h in range(HEADS):
        cols = slice(h * HD, (h + 1) * HD)
        q = jnp.concatenate([ref[:TILE, cols] for ref in q_refs], axis=0)
        k = jnp.concatenate([kv_refs[n][lo : lo + TILE, cols] for n, lo, _ in groups], axis=0)
        v = jnp.concatenate([kv_refs[n][lo + TILE : lo + 2 * TILE, cols] for n, lo, _ in groups], axis=0)
        scores = lax.dot_general(q, k, (((1,), (1,)), ((), ())), preferred_element_type=jnp.float32)
        shifted = jnp.concatenate(
            [
                jnp.concatenate(
                    [
                        scores[i * TILE : (i + 1) * TILE, j * TILE : (j + 1) * TILE] * FACTOR + bias[i][j]
                        for j in range(len(groups))
                    ],
                    axis=1,
                )
                for i in range(query_count)
            ],
            axis=0,
        )
        peak = jnp.max(shifted, axis=1, keepdims=True)
        if with_state:
            old_peak = old_stats[:, h : h + 1]
            peak = jnp.maximum(peak, old_peak)
        peak = peak.astype(jnp.bfloat16).astype(jnp.float32)
        unrounded = jnp.exp2(shifted - peak)
        total = jnp.sum(unrounded, axis=1, keepdims=True)
        summed = jnp.dot(unrounded.astype(jnp.bfloat16), v, preferred_element_type=jnp.float32)
        if with_state:
            factor = jnp.exp2(old_peak - peak)
            total = total + factor * old_stats[:, h + 8 : h + 9]
            summed = summed + factor * old_sum[:, cols]
        stats = jnp.where(lane == h, peak, stats)
        if message:
            high = total.astype(jnp.bfloat16).astype(jnp.float32)
            stats = jnp.where(lane == h + 8, high, stats)
            stats = jnp.where(lane == h + 16, total - high, stats)
            for i in range(query_count):
                refs[i][:, cols] = summed[i * TILE : (i + 1) * TILE].astype(jnp.bfloat16)
        else:
            stats = jnp.where(lane == h + 8, total, stats)
            refs[0][:, cols] = summed
    if message:
        for i in range(query_count):
            refs[i][:, FEAT:] = stats[i * TILE : (i + 1) * TILE].astype(jnp.bfloat16)
    else:
        refs[1][...] = stats


VMEM = pl.BlockSpec(memory_space=pltpu.VMEM)


def attention(queries, pieces, groups, state=None, message=False):
    count = len(queries)
    rows = count * TILE
    if message:
        out_shape = (jax.ShapeDtypeStruct((TILE, FEAT + HD), jnp.bfloat16),) * count
    else:
        out_shape = (
            jax.ShapeDtypeStruct((rows, FEAT), jnp.float32),
            jax.ShapeDtypeStruct((rows, HD), jnp.float32),
        )
    in_specs = [VMEM] * (count + len(pieces))
    operands = [*queries, *pieces]
    if state is not None:
        (total_rows, which), arrays = state
        for array in arrays:
            in_specs.append(pl.BlockSpec((rows, array.shape[1]), lambda i: (which, 0)))
            operands.append(array)
    pairs = count * len(groups)
    return pl.pallas_call(
        functools.partial(attention_kernel, groups, count, state is not None, message),
        grid=(1,),
        out_shape=out_shape,
        in_specs=in_specs,
        out_specs=(VMEM,) * len(out_shape),
        compiler_params=pltpu.CompilerParams(vmem_limit_bytes=12 * 1024 * 1024),
        cost_estimate=pl.CostEstimate(
            flops=60 * pairs * TILE * TILE * FEAT,
            bytes_accessed=len(groups) * 4 * TILE * FEAT,
            transcendentals=pairs * TILE * TILE * HEADS,
        ),
    )(*operands)


def stack_kernel(count, *refs):
    arrays, (out, done) = refs[:count], refs[count:]
    copies = []
    low = 0
    for n, ref in enumerate(arrays):
        copies.append(pltpu.make_async_copy(ref, out.at[pl.ds(low, ref.shape[0])], done.at[n]))
        copies[-1].start()
        low += ref.shape[0]
    for copy in copies:
        copy.wait()


def stacked(*arrays):
    rows = sum(a.shape[0] for a in arrays)
    anywhere = pl.BlockSpec(memory_space=pltpu.HBM if arrays[0].shape[0] == TILE else pl.ANY)
    return pl.pallas_call(
        functools.partial(stack_kernel, len(arrays)),
        out_shape=jax.ShapeDtypeStruct((rows, arrays[0].shape[1]), arrays[0].dtype),
        in_specs=[anywhere] * len(arrays),
        out_specs=pl.BlockSpec(memory_space=pl.ANY),
        scratch_shapes=[pltpu.SemaphoreType.DMA((len(arrays),))],
        compiler_params=pltpu.CompilerParams(vmem_limit_bytes=2**20),
        cost_estimate=pl.CostEstimate(flops=0, bytes_accessed=4 * rows * FEAT, transcendentals=0),
    )(*arrays)


def merge_kernel(o0, s0, op, om, out):
    own = s0[...]
    peaks, totals, sums = [own], [pltpu.roll(own, HD - 8, 1)], [o0]
    for ref in (op, om):
        stats = ref[:, FEAT:].astype(jnp.float32)
        total = pltpu.roll(stats, HD - 8, 1) + pltpu.roll(stats, HD - 16, 1)
        peaks.append(jnp.where(total > 0, stats, -1e30))
        totals.append(total)
        sums.append(ref)
    peak = jnp.maximum(jnp.maximum(peaks[0], peaks[1]), peaks[2])
    factors = [jnp.exp2(p - peak) for p in peaks]
    total = sum(f * t for f, t in zip(factors, totals))
    shares = [f / total for f in factors]
    for h in range(HEADS):
        cols = slice(h * HD, (h + 1) * HD)
        parts = [w[:, h : h + 1] * ref[:, cols].astype(jnp.float32) for w, ref in zip(shares, sums)]
        out[:, cols] = (parts[0] + parts[1] + parts[2]).astype(jnp.bfloat16)


def merge(*operands):
    return pl.pallas_call(
        merge_kernel,
        out_shape=jax.ShapeDtypeStruct((TILE, FEAT), jnp.bfloat16),
        in_specs=[VMEM] * len(operands),
        out_specs=VMEM,
        compiler_params=pltpu.CompilerParams(vmem_limit_bytes=12 * 1024 * 1024),
        cost_estimate=pl.CostEstimate(flops=10 * TILE * FEAT, bytes_accessed=2**20, transcendentals=0),
    )(*operands)


def project_kernel(_, rows, weight, out):
    product = lax.dot_general(
        rows[...], weight[...], (((1,), (1,)), ((), ())), preferred_element_type=jnp.float32
    )
    out[...] = product.astype(out.dtype)


def project(rows, weight, which, dtype):
    half = weight.shape[0] // 2
    return pl.pallas_call(
        project_kernel,
        grid_spec=pltpu.PrefetchScalarGridSpec(
            num_scalar_prefetch=1,
            grid=(1,),
            in_specs=[
                pl.BlockSpec(rows.shape, lambda i, c: (0, 0)),
                pl.BlockSpec((half, FEAT), lambda i, c: (c[0], 0)),
            ],
            out_specs=pl.BlockSpec((rows.shape[0], half), lambda i, c: (0, 0)),
        ),
        out_shape=jax.ShapeDtypeStruct((rows.shape[0], half), dtype),
        compiler_params=pltpu.CompilerParams(vmem_limit_bytes=12 * 1024 * 1024),
        cost_estimate=pl.CostEstimate(
            flops=2 * rows.shape[0] * half * FEAT, bytes_accessed=3 * 2**20, transcendentals=0
        ),
    )(which[None], rows, weight)


PAD = 16
SHARE = 12
WIDE = 8 * 4 * SHARE


def column_order():
    order = np.zeros((4, 8, PAD, WIDE), np.float32)
    for x in range(4):
        for p in range(8):
            for j in range(SHARE):
                order[x, p, j, (p * 4 + x) * SHARE + j] = 1
    return order.reshape(4 * HD, WIDE)


def arrange_kernel(pieces, order, out):
    for z in range(4):
        block = jnp.concatenate([pieces[x, :, z * HD : (z + 1) * HD] for x in range(4)], axis=1)
        product = jnp.dot(block, order[...], preferred_element_type=jnp.float32)
        out[:, z * WIDE : (z + 1) * WIDE] = product.astype(jnp.bfloat16)


def arrange(pieces):
    return pl.pallas_call(
        arrange_kernel,
        out_shape=jax.ShapeDtypeStruct((TILE, 4 * WIDE), jnp.bfloat16),
        in_specs=[VMEM, VMEM],
        out_specs=VMEM,
        compiler_params=pltpu.CompilerParams(vmem_limit_bytes=12 * 1024 * 1024),
        cost_estimate=pl.CostEstimate(flops=2 * TILE * 4 * HD * 4 * WIDE, bytes_accessed=2**20, transcendentals=0),
    )(pieces, jnp.asarray(column_order(), jnp.bfloat16))


def body(queries, keys, values, window, out_weight):
    my_tile = lax.axis_index(TOK)
    core = lax.axis_index("head")
    kv = stacked(keys, values)
    ap = lax.ppermute(kv, ALL, first_axis(1))
    am = lax.ppermute(kv, ALL, first_axis(-1))
    part = jnp.pad(out_weight.T, ((0, PAD - SHARE), (0, 0)))
    line_y = lax.all_to_all(jnp.broadcast_to(part, (8, PAD, FEAT)), "y", 0, 0)
    weight = lax.all_gather(line_y.reshape(-1, FEAT), "z", tiled=True)
    bias = biases(window, my_tile, core)
    q0 = with_biases(queries, bias[0])
    qp = lax.ppermute(with_biases(queries, bias[2]), ALL, row_axis(1))
    qm = lax.ppermute(with_biases(queries, bias[1]), ALL, row_axis(-1))
    line = stacked(kv, ap, am)
    bp = lax.ppermute(line, ALL, second_axis(1))
    bm = lax.ppermute(line, ALL, second_axis(-1))
    near = [(n, 0, 3 * n) for n in range(3)]
    far = [(n, 2 * TILE * a, 3 * a + n + 1) for n in range(2) for a in range(3)]
    state = attention((qp, qm, q0), (kv, ap, am), near)
    op, om = attention((qp, qm), (bp, bm), far, ((3, 0), state), message=True)
    back_p = lax.ppermute(om, ALL, row_axis(1))
    back_m = lax.ppermute(op, ALL, row_axis(-1))
    o0, s0 = attention((q0,), (bp, bm), far, ((3, 2), state))
    attended = merge(o0, s0, back_p, back_m)
    rows = lax.all_gather(attended, "x", tiled=True)
    other = project(rows, weight, 1 - core, jnp.bfloat16)
    received = lax.ppermute(other, "head", [(0, 1), (1, 0)])
    mine = project(rows, weight, core, jnp.float32)
    columns = (mine + received.astype(jnp.float32)).astype(jnp.bfloat16)
    pieces = lax.all_to_all(columns.reshape(4, TILE, -1), "x", 0, 0)
    return arrange(pieces)


def solution(mesh):
    fine = Mesh(mesh.devices.reshape(8, 8, 4, 2), ALL)
    in_specs = (P(TOK, "head"), P(TOK, "head"), P(TOK, "head"), P(TOK, None), P("head", TOK))
    return jax.shard_map(body, mesh=fine, in_specs=in_specs, out_specs=P(TOK, "head"), check_vma=False)
```

```python
import functools

import jax
import jax.numpy as jnp
import numpy as np
from jax import lax
from jax.experimental import pallas as pl
from jax.experimental.pallas import tpu as pltpu
from jax.sharding import Mesh, PartitionSpec as P

HD = 128
TILE = 128
HEADS = 6
FEAT = HEADS * HD
TF, TH, TW = 8, 4, 8
TILES = TF * TH * TW
ALL = ("z", "y", "x", "head")
TOK = ("z", "y", "x")
FACTOR = float(HD**-0.5 * np.log2(np.e))
OFFSETS = (0, 1, -1)
FLAG_ROWS = 16


def place(tile):
    return tile // (TH * TW), tile // TW % TH, tile % TW


def from_neighbour(offset_of_core):
    pairs = []
    for tile in range(TILES):
        for core in range(2):
            f, r, c = (a + b for a, b in zip(place(tile), offset_of_core(core)))
            if 0 <= f < TF and 0 <= r < TH and 0 <= c < TW:
                source = (f * TH + r) * TW + c
                pairs.append((2 * source + core, 2 * tile + core))
    return pairs


def first_axis(step):
    return from_neighbour(lambda core: (step, 0, 0) if core == 0 else (0, 0, step))


def second_axis(step):
    return from_neighbour(lambda core: (0, 0, step) if core == 0 else (step, 0, 0))


def row_axis(step):
    return from_neighbour(lambda core: (0, step, 0))


def biases(window, my_tile, core):
    slot = jnp.arange(27, dtype=jnp.int32)

    def step(digit):
        return jnp.where(digit == 2, -1, digit)

    dr, da, db = step(slot // 9), step(slot // 3 % 3), step(slot % 3)
    df = jnp.where(core == 0, da, db)
    dc = jnp.where(core == 0, db, da)
    f, r, c = place(my_tile)
    inside = (
        (f + df >= 0) & (f + df < TF) & (r + dr >= 0) & (r + dr < TH) & (c + dc >= 0) & (c + dc < TW)
    )
    tile = my_tile + (df * TH + dr) * TW + dc
    listed = inside & jnp.any(window[0][None, :] == tile[:, None], axis=1)
    return jnp.where(listed, 0.0, -1e30).astype(jnp.bfloat16).reshape(3, 9)


def with_biases(queries, bias):
    rows = jnp.zeros((FLAG_ROWS,), jnp.bfloat16).at[:9].set(bias)
    return jnp.concatenate([queries, jnp.broadcast_to(rows[:, None], (FLAG_ROWS, queries.shape[1]))])


def attention_kernel(groups, query_count, with_state, message, *refs):
    refs = list(refs)
    q_refs = [refs.pop(0) for _ in range(query_count)]
    kv_refs = [refs.pop(0) for _ in range(max(g[0] for g in groups) + 1)]
    old_sum, old_stats = (refs.pop(0), refs.pop(0)) if with_state else (None, None)
    rows = query_count * TILE
    bias = []
    for ref in q_refs:
        block = ref[TILE : TILE + FLAG_ROWS, :HD].astype(jnp.float32)
        bias.append([block[j : j + 1, :] for _, _, j in groups])
    lane = lax.broadcasted_iota(jnp.int32, (rows, HD), 1)
    stats = jnp.zeros((rows, HD), jnp.float32)
    for h in range(HEADS):
        cols = slice(h * HD, (h + 1) * HD)
        q = jnp.concatenate([ref[:TILE, cols] for ref in q_refs], axis=0)
        k = jnp.concatenate([kv_refs[n][lo : lo + TILE, cols] for n, lo, _ in groups], axis=0)
        v = jnp.concatenate([kv_refs[n][lo + TILE : lo + 2 * TILE, cols] for n, lo, _ in groups], axis=0)
        scores = lax.dot_general(q, k, (((1,), (1,)), ((), ())), preferred_element_type=jnp.float32)
        shifted = jnp.concatenate(
            [
                jnp.concatenate(
                    [
                        scores[i * TILE : (i + 1) * TILE, j * TILE : (j + 1) * TILE] * FACTOR + bias[i][j]
                        for j in range(len(groups))
                    ],
                    axis=1,
                )
                for i in range(query_count)
            ],
            axis=0,
        )
        peak = jnp.max(shifted, axis=1, keepdims=True)
        if with_state:
            old_peak = old_stats[:, h : h + 1]
            peak = jnp.maximum(peak, old_peak)
        peak = peak.astype(jnp.bfloat16).astype(jnp.float32)
        unrounded = jnp.exp2(shifted - peak)
        total = jnp.sum(unrounded, axis=1, keepdims=True)
        summed = jnp.dot(unrounded.astype(jnp.bfloat16), v, preferred_element_type=jnp.float32)
        if with_state:
            factor = jnp.exp2(old_peak - peak)
            total = total + factor * old_stats[:, h + 8 : h + 9]
            summed = summed + factor * old_sum[:, cols]
        stats = jnp.where(lane == h, peak, stats)
        if message:
            high = total.astype(jnp.bfloat16).astype(jnp.float32)
            stats = jnp.where(lane == h + 8, high, stats)
            stats = jnp.where(lane == h + 16, total - high, stats)
            for i in range(query_count):
                refs[i][:, cols] = summed[i * TILE : (i + 1) * TILE].astype(jnp.bfloat16)
        else:
            stats = jnp.where(lane == h + 8, total, stats)
            refs[0][:, cols] = summed
    if message:
        for i in range(query_count):
            refs[i][:, FEAT:] = stats[i * TILE : (i + 1) * TILE].astype(jnp.bfloat16)
    else:
        refs[1][...] = stats


VMEM = pl.BlockSpec(memory_space=pltpu.VMEM)


def attention(queries, pieces, groups, state=None, message=False):
    count = len(queries)
    rows = count * TILE
    if message:
        out_shape = (jax.ShapeDtypeStruct((TILE, FEAT + HD), jnp.bfloat16),) * count
    else:
        out_shape = (
            jax.ShapeDtypeStruct((rows, FEAT), jnp.float32),
            jax.ShapeDtypeStruct((rows, HD), jnp.float32),
        )
    in_specs = [VMEM] * (count + len(pieces))
    operands = [*queries, *pieces]
    if state is not None:
        (total_rows, which), arrays = state
        for array in arrays:
            in_specs.append(pl.BlockSpec((rows, array.shape[1]), lambda i: (which, 0)))
            operands.append(array)
    pairs = count * len(groups)
    return pl.pallas_call(
        functools.partial(attention_kernel, groups, count, state is not None, message),
        grid=(1,),
        out_shape=out_shape,
        in_specs=in_specs,
        out_specs=(VMEM,) * len(out_shape),
        compiler_params=pltpu.CompilerParams(vmem_limit_bytes=12 * 1024 * 1024),
        cost_estimate=pl.CostEstimate(
            flops=36 * pairs * TILE * TILE * FEAT,
            bytes_accessed=len(groups) * 4 * TILE * FEAT,
            transcendentals=pairs * TILE * TILE * HEADS,
        ),
    )(*operands)


def stack_kernel(count, *refs):
    arrays, (out, done) = refs[:count], refs[count:]
    copies = []
    low = 0
    for n, ref in enumerate(arrays):
        copies.append(pltpu.make_async_copy(ref, out.at[pl.ds(low, ref.shape[0])], done.at[n]))
        copies[-1].start()
        low += ref.shape[0]
    for copy in copies:
        copy.wait()


def stacked(vmem_limit, *arrays):
    rows = sum(a.shape[0] for a in arrays)
    anywhere = pl.BlockSpec(memory_space=pltpu.HBM if arrays[0].shape[0] == TILE else pl.ANY)
    return pl.pallas_call(
        functools.partial(stack_kernel, len(arrays)),
        out_shape=jax.ShapeDtypeStruct((rows, arrays[0].shape[1]), arrays[0].dtype),
        in_specs=[anywhere] * len(arrays),
        out_specs=pl.BlockSpec(memory_space=pl.ANY),
        scratch_shapes=[pltpu.SemaphoreType.DMA((len(arrays),))],
        compiler_params=pltpu.CompilerParams(vmem_limit_bytes=vmem_limit),
        cost_estimate=pl.CostEstimate(flops=0, bytes_accessed=4 * rows * FEAT, transcendentals=0),
    )(*arrays)


def merge_kernel(o0, s0, op, om, out):
    own = s0[...]
    peaks, totals, sums = [own], [pltpu.roll(own, HD - 8, 1)], [o0]
    for ref in (op, om):
        stats = ref[:, FEAT:].astype(jnp.float32)
        total = pltpu.roll(stats, HD - 8, 1) + pltpu.roll(stats, HD - 16, 1)
        peaks.append(jnp.where(total > 0, stats, -1e30))
        totals.append(total)
        sums.append(ref)
    peak = jnp.maximum(jnp.maximum(peaks[0], peaks[1]), peaks[2])
    factors = [jnp.exp2(p - peak) for p in peaks]
    total = sum(f * t for f, t in zip(factors, totals))
    shares = [f / total for f in factors]
    for h in range(HEADS):
        cols = slice(h * HD, (h + 1) * HD)
        parts = [w[:, h : h + 1] * ref[:, cols].astype(jnp.float32) for w, ref in zip(shares, sums)]
        out[:, cols] = (parts[0] + parts[1] + parts[2]).astype(jnp.bfloat16)


def merge(*operands):
    return pl.pallas_call(
        merge_kernel,
        out_shape=jax.ShapeDtypeStruct((TILE, FEAT), jnp.bfloat16),
        in_specs=[VMEM] * len(operands),
        out_specs=VMEM,
        compiler_params=pltpu.CompilerParams(vmem_limit_bytes=12 * 1024 * 1024),
        cost_estimate=pl.CostEstimate(flops=10 * TILE * FEAT, bytes_accessed=2**20, transcendentals=0),
    )(*operands)


def project_kernel(_, rows, weight, out):
    product = lax.dot_general(
        rows[...], weight[...], (((1,), (1,)), ((), ())), preferred_element_type=jnp.float32
    )
    out[...] = product.astype(out.dtype)


def project(rows, weight, which, dtype):
    half = weight.shape[0] // 2
    return pl.pallas_call(
        project_kernel,
        grid_spec=pltpu.PrefetchScalarGridSpec(
            num_scalar_prefetch=1,
            grid=(1,),
            in_specs=[
                pl.BlockSpec(rows.shape, lambda i, c: (0, 0)),
                pl.BlockSpec((half, FEAT), lambda i, c: (c[0], 0)),
            ],
            out_specs=pl.BlockSpec((rows.shape[0], half), lambda i, c: (0, 0)),
        ),
        out_shape=jax.ShapeDtypeStruct((rows.shape[0], half), dtype),
        compiler_params=pltpu.CompilerParams(vmem_limit_bytes=12 * 1024 * 1024),
        cost_estimate=pl.CostEstimate(
            flops=2 * rows.shape[0] * half * FEAT, bytes_accessed=3 * 2**20, transcendentals=0
        ),
    )(which[None], rows, weight)


PAD = 16
SHARE = 12
WIDE = 8 * 4 * SHARE


def column_order():
    order = np.zeros((4, 8, PAD, WIDE), np.float32)
    for x in range(4):
        for p in range(8):
            for j in range(SHARE):
                order[x, p, j, (p * 4 + x) * SHARE + j] = 1
    return order.reshape(4 * HD, WIDE)


def arrange_kernel(pieces, order, out):
    for z in range(4):
        block = jnp.concatenate([pieces[x, :, z * HD : (z + 1) * HD] for x in range(4)], axis=1)
        product = jnp.dot(block, order[...], preferred_element_type=jnp.float32)
        out[:, z * WIDE : (z + 1) * WIDE] = product.astype(jnp.bfloat16)


def arrange(pieces):
    return pl.pallas_call(
        arrange_kernel,
        out_shape=jax.ShapeDtypeStruct((TILE, 4 * WIDE), jnp.bfloat16),
        in_specs=[VMEM, VMEM],
        out_specs=VMEM,
        compiler_params=pltpu.CompilerParams(vmem_limit_bytes=12 * 1024 * 1024),
        cost_estimate=pl.CostEstimate(flops=2 * TILE * 4 * HD * 4 * WIDE, bytes_accessed=2**20, transcendentals=0),
    )(pieces, jnp.asarray(column_order(), jnp.bfloat16))


def body(queries, keys, values, window, out_weight):
    my_tile = lax.axis_index(TOK)
    core = lax.axis_index("head")
    kv = stacked(56 * 2**20, keys, values)
    ap = lax.ppermute(kv, ALL, first_axis(1))
    am = lax.ppermute(kv, ALL, first_axis(-1))
    part = jnp.pad(out_weight.T, ((0, PAD - SHARE), (0, 0)))
    weight = lax.all_gather(part, ("z", "y"), tiled=True)
    bias = biases(window, my_tile, core)
    q0 = with_biases(queries, bias[0])
    qp = lax.ppermute(with_biases(queries, bias[2]), ALL, row_axis(1))
    qm = lax.ppermute(with_biases(queries, bias[1]), ALL, row_axis(-1))
    line = stacked(2**20, kv, ap, am)
    bp = lax.ppermute(line, ALL, second_axis(1))
    bm = lax.ppermute(line, ALL, second_axis(-1))
    near = [(n, 0, 3 * n) for n in range(3)]
    far = [(n, 2 * TILE * a, 3 * a + n + 1) for n in range(2) for a in range(3)]
    state = attention((qp, qm, q0), (kv, ap, am), near)
    op, om = attention((qp, qm), (bp, bm), far, ((3, 0), state), message=True)
    back_p = lax.ppermute(om, ALL, row_axis(1))
    back_m = lax.ppermute(op, ALL, row_axis(-1))
    o0, s0 = attention((q0,), (bp, bm), far, ((3, 2), state))
    attended = merge(o0, s0, back_p, back_m)
    rows = lax.all_gather(attended, "x", tiled=True)
    other = project(rows, weight, 1 - core, jnp.bfloat16)
    received = lax.ppermute(other, "head", [(0, 1), (1, 0)])
    mine = project(rows, weight, core, jnp.float32)
    columns = (mine + received.astype(jnp.float32)).astype(jnp.bfloat16)
    pieces = lax.all_to_all(columns.reshape(4, TILE, -1), "x", 0, 0)
    return arrange(pieces)


def solution(mesh):
    fine = Mesh(mesh.devices.reshape(8, 8, 4, 2), ALL)
    in_specs = (P(TOK, "head"), P(TOK, "head"), P(TOK, "head"), P(TOK, None), P("head", TOK))
    return jax.shard_map(body, mesh=fine, in_specs=in_specs, out_specs=P(TOK, "head"), check_vma=False)
```

```python
import functools

import jax
import jax.numpy as jnp
import numpy as np
from jax import lax
from jax.experimental import pallas as pl
from jax.experimental.pallas import tpu as pltpu
from jax.sharding import Mesh, PartitionSpec as P

HD = 128
TILE = 128
HEADS = 6
FEAT = HEADS * HD
TF, TH, TW = 8, 4, 8
TILES = TF * TH * TW
ALL = ("z", "y", "x", "head")
TOK = ("z", "y", "x")
FACTOR = float(HD**-0.5 * np.log2(np.e))
OFFSETS = (0, 1, -1)
FLAG_ROWS = 16


def place(tile):
    return tile // (TH * TW), tile // TW % TH, tile % TW


def from_neighbour(offset_of_core):
    pairs = []
    for tile in range(TILES):
        for core in range(2):
            f, r, c = (a + b for a, b in zip(place(tile), offset_of_core(core)))
            if 0 <= f < TF and 0 <= r < TH and 0 <= c < TW:
                source = (f * TH + r) * TW + c
                pairs.append((2 * source + core, 2 * tile + core))
    return pairs


def first_axis(step):
    return from_neighbour(lambda core: (step, 0, 0) if core == 0 else (0, 0, step))


def second_axis(step):
    return from_neighbour(lambda core: (0, 0, step) if core == 0 else (step, 0, 0))


def row_axis(step):
    return from_neighbour(lambda core: (0, step, 0))


def biases(window, my_tile, core):
    slot = jnp.arange(27, dtype=jnp.int32)

    def step(digit):
        return jnp.where(digit == 2, -1, digit)

    dr, da, db = step(slot // 9), step(slot // 3 % 3), step(slot % 3)
    df = jnp.where(core == 0, da, db)
    dc = jnp.where(core == 0, db, da)
    f, r, c = place(my_tile)
    inside = (
        (f + df >= 0) & (f + df < TF) & (r + dr >= 0) & (r + dr < TH) & (c + dc >= 0) & (c + dc < TW)
    )
    tile = my_tile + (df * TH + dr) * TW + dc
    listed = inside & jnp.any(window[0][None, :] == tile[:, None], axis=1)
    return jnp.where(listed, 0.0, -1e30).astype(jnp.bfloat16).reshape(3, 9)


def with_biases(queries, bias):
    rows = jnp.zeros((FLAG_ROWS,), jnp.bfloat16).at[:9].set(bias)
    return jnp.concatenate([queries, jnp.broadcast_to(rows[:, None], (FLAG_ROWS, queries.shape[1]))])


def attention_kernel(groups, query_count, with_state, message, *refs):
    refs = list(refs)
    q_refs = [refs.pop(0) for _ in range(query_count)]
    kv_refs = [refs.pop(0) for _ in range(max(g[0] for g in groups) + 1)]
    old_sum, old_stats = (refs.pop(0), refs.pop(0)) if with_state else (None, None)
    rows = query_count * TILE
    bias = []
    for ref in q_refs:
        block = ref[TILE : TILE + FLAG_ROWS, :HD].astype(jnp.float32)
        bias.append([block[j : j + 1, :] for _, _, j in groups])
    lane = lax.broadcasted_iota(jnp.int32, (rows, HD), 1)
    stats = jnp.zeros((rows, HD), jnp.float32)
    for h in range(HEADS):
        cols = slice(h * HD, (h + 1) * HD)
        q = jnp.concatenate([ref[:TILE, cols] for ref in q_refs], axis=0)
        k = jnp.concatenate([kv_refs[n][lo : lo + TILE, cols] for n, lo, _ in groups], axis=0)
        v = jnp.concatenate([kv_refs[n][lo + TILE : lo + 2 * TILE, cols] for n, lo, _ in groups], axis=0)
        scores = lax.dot_general(q, k, (((1,), (1,)), ((), ())), preferred_element_type=jnp.float32)
        shifted = jnp.concatenate(
            [
                jnp.concatenate(
                    [
                        scores[i * TILE : (i + 1) * TILE, j * TILE : (j + 1) * TILE] * FACTOR + bias[i][j]
                        for j in range(len(groups))
                    ],
                    axis=1,
                )
                for i in range(query_count)
            ],
            axis=0,
        )
        peak = jnp.max(shifted, axis=1, keepdims=True)
        if with_state:
            old_peak = old_stats[:, h : h + 1]
            peak = jnp.maximum(peak, old_peak)
        peak = peak.astype(jnp.bfloat16).astype(jnp.float32)
        unrounded = jnp.exp2(shifted - peak)
        total = jnp.sum(unrounded, axis=1, keepdims=True)
        summed = jnp.dot(unrounded.astype(jnp.bfloat16), v, preferred_element_type=jnp.float32)
        if with_state:
            factor = jnp.exp2(old_peak - peak)
            total = total + factor * old_stats[:, h + 8 : h + 9]
            summed = summed + factor * old_sum[:, cols]
        stats = jnp.where(lane == h, peak, stats)
        if message:
            high = total.astype(jnp.bfloat16).astype(jnp.float32)
            stats = jnp.where(lane == h + 8, high, stats)
            stats = jnp.where(lane == h + 16, total - high, stats)
            for i in range(query_count):
                refs[i][:, cols] = summed[i * TILE : (i + 1) * TILE].astype(jnp.bfloat16)
        else:
            stats = jnp.where(lane == h + 8, total, stats)
            refs[0][:, cols] = summed
    if message:
        for i in range(query_count):
            refs[i][:, FEAT:] = stats[i * TILE : (i + 1) * TILE].astype(jnp.bfloat16)
    else:
        refs[1][...] = stats


VMEM = pl.BlockSpec(memory_space=pltpu.VMEM)


def attention(queries, pieces, groups, state=None, message=False):
    count = len(queries)
    rows = count * TILE
    if message:
        out_shape = (jax.ShapeDtypeStruct((TILE, FEAT + HD), jnp.bfloat16),) * count
    else:
        out_shape = (
            jax.ShapeDtypeStruct((rows, FEAT), jnp.float32),
            jax.ShapeDtypeStruct((rows, HD), jnp.float32),
        )
    in_specs = [VMEM] * (count + len(pieces))
    operands = [*queries, *pieces]
    if state is not None:
        (total_rows, which), arrays = state
        for array in arrays:
            in_specs.append(pl.BlockSpec((rows, array.shape[1]), lambda i: (which, 0)))
            operands.append(array)
    pairs = count * len(groups)
    return pl.pallas_call(
        functools.partial(attention_kernel, groups, count, state is not None, message),
        grid=(1,),
        out_shape=out_shape,
        in_specs=in_specs,
        out_specs=(VMEM,) * len(out_shape),
        compiler_params=pltpu.CompilerParams(vmem_limit_bytes=12 * 1024 * 1024),
        cost_estimate=pl.CostEstimate(
            flops=60 * pairs * TILE * TILE * FEAT,
            bytes_accessed=len(groups) * 4 * TILE * FEAT,
            transcendentals=pairs * TILE * TILE * HEADS,
        ),
    )(*operands)


def stack_kernel(count, *refs):
    arrays, (out, done) = refs[:count], refs[count:]
    copies = []
    low = 0
    for n, ref in enumerate(arrays):
        copies.append(pltpu.make_async_copy(ref, out.at[pl.ds(low, ref.shape[0])], done.at[n]))
        copies[-1].start()
        low += ref.shape[0]
    for copy in copies:
        copy.wait()


def stacked(*arrays):
    rows = sum(a.shape[0] for a in arrays)
    anywhere = pl.BlockSpec(memory_space=pltpu.HBM if arrays[0].shape[0] == TILE else pl.ANY)
    return pl.pallas_call(
        functools.partial(stack_kernel, len(arrays)),
        out_shape=jax.ShapeDtypeStruct((rows, arrays[0].shape[1]), arrays[0].dtype),
        in_specs=[anywhere] * len(arrays),
        out_specs=pl.BlockSpec(memory_space=pl.ANY),
        scratch_shapes=[pltpu.SemaphoreType.DMA((len(arrays),))],
        compiler_params=pltpu.CompilerParams(vmem_limit_bytes=2**20),
        cost_estimate=pl.CostEstimate(flops=0, bytes_accessed=4 * rows * FEAT, transcendentals=0),
    )(*arrays)


def merge_kernel(o0, s0, op, om, out):
    own = s0[...]
    peaks, totals, sums = [own], [pltpu.roll(own, HD - 8, 1)], [o0]
    for ref in (op, om):
        stats = ref[:, FEAT:].astype(jnp.float32)
        total = pltpu.roll(stats, HD - 8, 1) + pltpu.roll(stats, HD - 16, 1)
        peaks.append(jnp.where(total > 0, stats, -1e30))
        totals.append(total)
        sums.append(ref)
    peak = jnp.maximum(jnp.maximum(peaks[0], peaks[1]), peaks[2])
    factors = [jnp.exp2(p - peak) for p in peaks]
    total = sum(f * t for f, t in zip(factors, totals))
    shares = [f / total for f in factors]
    for h in range(HEADS):
        cols = slice(h * HD, (h + 1) * HD)
        parts = [w[:, h : h + 1] * ref[:, cols].astype(jnp.float32) for w, ref in zip(shares, sums)]
        out[:, cols] = (parts[0] + parts[1] + parts[2]).astype(jnp.bfloat16)


def merge(*operands):
    return pl.pallas_call(
        merge_kernel,
        out_shape=jax.ShapeDtypeStruct((TILE, FEAT), jnp.bfloat16),
        in_specs=[VMEM] * len(operands),
        out_specs=VMEM,
        compiler_params=pltpu.CompilerParams(vmem_limit_bytes=12 * 1024 * 1024),
        cost_estimate=pl.CostEstimate(flops=10 * TILE * FEAT, bytes_accessed=2**20, transcendentals=0),
    )(*operands)


def project_kernel(_, rows, weight, out):
    product = lax.dot_general(
        rows[...], weight[...], (((1,), (1,)), ((), ())), preferred_element_type=jnp.float32
    )
    out[...] = product.astype(out.dtype)


def project(rows, weight, which, dtype):
    half = weight.shape[0] // 2
    return pl.pallas_call(
        project_kernel,
        grid_spec=pltpu.PrefetchScalarGridSpec(
            num_scalar_prefetch=1,
            grid=(1,),
            in_specs=[
                pl.BlockSpec(rows.shape, lambda i, c: (0, 0)),
                pl.BlockSpec((half, FEAT), lambda i, c: (c[0], 0)),
            ],
            out_specs=pl.BlockSpec((rows.shape[0], half), lambda i, c: (0, 0)),
        ),
        out_shape=jax.ShapeDtypeStruct((rows.shape[0], half), dtype),
        compiler_params=pltpu.CompilerParams(vmem_limit_bytes=12 * 1024 * 1024),
        cost_estimate=pl.CostEstimate(
            flops=2 * rows.shape[0] * half * FEAT, bytes_accessed=3 * 2**20, transcendentals=0
        ),
    )(which[None], rows, weight)


PAD = 16
SHARE = 12
WIDE = 8 * 4 * SHARE


def column_order():
    order = np.zeros((4, 8, PAD, WIDE), np.float32)
    for x in range(4):
        for p in range(8):
            for j in range(SHARE):
                order[x, p, j, (p * 4 + x) * SHARE + j] = 1
    return order.reshape(4 * HD, WIDE)


def arrange_kernel(pieces, order, out):
    for z in range(4):
        block = jnp.concatenate([pieces[x, :, z * HD : (z + 1) * HD] for x in range(4)], axis=1)
        product = jnp.dot(block, order[...], preferred_element_type=jnp.float32)
        out[:, z * WIDE : (z + 1) * WIDE] = product.astype(jnp.bfloat16)


def arrange(pieces):
    return pl.pallas_call(
        arrange_kernel,
        out_shape=jax.ShapeDtypeStruct((TILE, 4 * WIDE), jnp.bfloat16),
        in_specs=[VMEM, VMEM],
        out_specs=VMEM,
        compiler_params=pltpu.CompilerParams(vmem_limit_bytes=12 * 1024 * 1024),
        cost_estimate=pl.CostEstimate(flops=2 * TILE * 4 * HD * 4 * WIDE, bytes_accessed=2**20, transcendentals=0),
    )(pieces, jnp.asarray(column_order(), jnp.bfloat16))


def body(queries, keys, values, window, out_weight):
    my_tile = lax.axis_index(TOK)
    core = lax.axis_index("head")
    kv = stacked(keys, values)
    ap = lax.ppermute(kv, ALL, first_axis(1))
    am = lax.ppermute(kv, ALL, first_axis(-1))
    line_y = lax.all_to_all(jnp.broadcast_to(out_weight.T, (8, SHARE, FEAT)), "y", 0, 0)
    bias = biases(window, my_tile, core)
    q0 = with_biases(queries, bias[0])
    qp = lax.ppermute(with_biases(queries, bias[2]), ALL, row_axis(1))
    qm = lax.ppermute(with_biases(queries, bias[1]), ALL, row_axis(-1))
    line = stacked(kv, ap, am)
    line_y, _ = lax.optimization_barrier((line_y, line))
    line_y = jnp.pad(line_y, ((0, 0), (0, PAD - SHARE), (0, 0)))
    weight = lax.all_gather(line_y.reshape(-1, FEAT), "z", tiled=True)
    bp = lax.ppermute(line, ALL, second_axis(1))
    bm = lax.ppermute(line, ALL, second_axis(-1))
    near = [(n, 0, 3 * n) for n in range(3)]
    far = [(n, 2 * TILE * a, 3 * a + n + 1) for n in range(2) for a in range(3)]
    state = attention((qp, qm, q0), (kv, ap, am), near)
    op, om = attention((qp, qm), (bp, bm), far, ((3, 0), state), message=True)
    back_p = lax.ppermute(om, ALL, row_axis(1))
    back_m = lax.ppermute(op, ALL, row_axis(-1))
    o0, s0 = attention((q0,), (bp, bm), far, ((3, 2), state))
    attended = merge(o0, s0, back_p, back_m)
    rows = lax.all_gather(attended, "x", tiled=True)
    other = project(rows, weight, 1 - core, jnp.bfloat16)
    received = lax.ppermute(other, "head", [(0, 1), (1, 0)])
    mine = project(rows, weight, core, jnp.float32)
    columns = (mine + received.astype(jnp.float32)).astype(jnp.bfloat16)
    pieces = lax.all_to_all(columns.reshape(4, TILE, -1), "x", 0, 0)
    return arrange(pieces)


def solution(mesh):
    fine = Mesh(mesh.devices.reshape(8, 8, 4, 2), ALL)
    in_specs = (P(TOK, "head"), P(TOK, "head"), P(TOK, "head"), P(TOK, None), P("head", TOK))
    return jax.shard_map(body, mesh=fine, in_specs=in_specs, out_specs=P(TOK, "head"), check_vma=False)
```

```python
import functools

import jax
import jax.numpy as jnp
import numpy as np
from jax import lax
from jax.experimental import pallas as pl
from jax.experimental.pallas import tpu as pltpu
from jax.sharding import Mesh, PartitionSpec as P

HD = 128
TILE = 128
HEADS = 6
FEAT = HEADS * HD
TF, TH, TW = 8, 4, 8
TILES = TF * TH * TW
ALL = ("z", "y", "x", "head")
TOK = ("z", "y", "x")
FACTOR = float(HD**-0.5 * np.log2(np.e))
OFFSETS = (0, 1, -1)
FLAG_ROWS = 16


def place(tile):
    return tile // (TH * TW), tile // TW % TH, tile % TW


def from_neighbour(offset_of_core):
    pairs = []
    for tile in range(TILES):
        for core in range(2):
            f, r, c = (a + b for a, b in zip(place(tile), offset_of_core(core)))
            if 0 <= f < TF and 0 <= r < TH and 0 <= c < TW:
                source = (f * TH + r) * TW + c
                pairs.append((2 * source + core, 2 * tile + core))
    return pairs


def first_axis(step):
    return from_neighbour(lambda core: (step, 0, 0) if core == 0 else (0, 0, step))


def second_axis(step):
    return from_neighbour(lambda core: (0, 0, step) if core == 0 else (step, 0, 0))


def row_axis(step):
    return from_neighbour(lambda core: (0, step, 0))


def biases(window, my_tile, core):
    slot = jnp.arange(27, dtype=jnp.int32)

    def step(digit):
        return jnp.where(digit == 2, -1, digit)

    dr, da, db = step(slot // 9), step(slot // 3 % 3), step(slot % 3)
    df = jnp.where(core == 0, da, db)
    dc = jnp.where(core == 0, db, da)
    f, r, c = place(my_tile)
    inside = (
        (f + df >= 0) & (f + df < TF) & (r + dr >= 0) & (r + dr < TH) & (c + dc >= 0) & (c + dc < TW)
    )
    tile = my_tile + (df * TH + dr) * TW + dc
    listed = inside & jnp.any(window[0][None, :] == tile[:, None], axis=1)
    return jnp.where(listed, 0.0, -1e30).astype(jnp.bfloat16).reshape(3, 9)


def with_biases(queries, bias):
    rows = jnp.zeros((FLAG_ROWS,), jnp.bfloat16).at[:9].set(bias)
    return jnp.concatenate([queries, jnp.broadcast_to(rows[:, None], (FLAG_ROWS, queries.shape[1]))])


def attention_kernel(groups, query_count, with_state, message, *refs):
    refs = list(refs)
    q_refs = [refs.pop(0) for _ in range(query_count)]
    kv_refs = [refs.pop(0) for _ in range(max(g[0] for g in groups) + 1)]
    old_sum, old_stats = (refs.pop(0), refs.pop(0)) if with_state else (None, None)
    rows = query_count * TILE
    bias = []
    for ref in q_refs:
        block = ref[TILE : TILE + FLAG_ROWS, :HD].astype(jnp.float32)
        bias.append([block[j : j + 1, :] for _, _, j in groups])
    lane = lax.broadcasted_iota(jnp.int32, (rows, HD), 1)
    stats = jnp.zeros((rows, HD), jnp.float32)
    for h in range(HEADS):
        cols = slice(h * HD, (h + 1) * HD)
        q = jnp.concatenate([ref[:TILE, cols] for ref in q_refs], axis=0)
        k = jnp.concatenate([kv_refs[n][lo : lo + TILE, cols] for n, lo, _ in groups], axis=0)
        v = jnp.concatenate([kv_refs[n][lo + TILE : lo + 2 * TILE, cols] for n, lo, _ in groups], axis=0)
        scores = lax.dot_general(q, k, (((1,), (1,)), ((), ())), preferred_element_type=jnp.float32)
        shifted = jnp.concatenate(
            [
                jnp.concatenate(
                    [
                        scores[i * TILE : (i + 1) * TILE, j * TILE : (j + 1) * TILE] * FACTOR + bias[i][j]
                        for j in range(len(groups))
                    ],
                    axis=1,
                )
                for i in range(query_count)
            ],
            axis=0,
        )
        peak = jnp.max(shifted, axis=1, keepdims=True)
        if with_state:
            old_peak = old_stats[:, h : h + 1]
            peak = jnp.maximum(peak, old_peak)
        peak = peak.astype(jnp.bfloat16).astype(jnp.float32)
        unrounded = jnp.exp2(shifted - peak)
        total = jnp.sum(unrounded, axis=1, keepdims=True)
        summed = jnp.dot(unrounded.astype(jnp.bfloat16), v, preferred_element_type=jnp.float32)
        if with_state:
            factor = jnp.exp2(old_peak - peak)
            total = total + factor * old_stats[:, h + 8 : h + 9]
            summed = summed + factor * old_sum[:, cols]
        stats = jnp.where(lane == h, peak, stats)
        if message:
            high = total.astype(jnp.bfloat16).astype(jnp.float32)
            stats = jnp.where(lane == h + 8, high, stats)
            stats = jnp.where(lane == h + 16, total - high, stats)
            for i in range(query_count):
                refs[i][:, cols] = summed[i * TILE : (i + 1) * TILE].astype(jnp.bfloat16)
        else:
            stats = jnp.where(lane == h + 8, total, stats)
            low = 0
            for ref in refs[::2]:
                ref[:, cols] = summed[low : low + ref.shape[0]]
                low += ref.shape[0]
    if message:
        for i in range(query_count):
            refs[i][:, FEAT:] = stats[i * TILE : (i + 1) * TILE].astype(jnp.bfloat16)
    else:
        low = 0
        for ref in refs[1::2]:
            ref[...] = stats[low : low + ref.shape[0]]
            low += ref.shape[0]


VMEM = pl.BlockSpec(memory_space=pltpu.VMEM)


def attention(queries, pieces, groups, state=(), message=False, parts=None):
    count = len(queries)
    if message:
        out_shape = (jax.ShapeDtypeStruct((TILE, FEAT + HD), jnp.bfloat16),) * count
    else:
        out_shape = tuple(
            jax.ShapeDtypeStruct((part * TILE, width), jnp.float32)
            for part in parts or (count,)
            for width in (FEAT, HD)
        )
    operands = (*queries, *pieces, *state)
    pairs = count * len(groups)
    return pl.pallas_call(
        functools.partial(attention_kernel, groups, count, bool(state), message),
        out_shape=out_shape,
        in_specs=[VMEM] * len(operands),
        out_specs=(VMEM,) * len(out_shape),
        compiler_params=pltpu.CompilerParams(vmem_limit_bytes=12 * 1024 * 1024),
        cost_estimate=pl.CostEstimate(
            flops=60 * pairs * TILE * TILE * FEAT,
            bytes_accessed=len(groups) * 4 * TILE * FEAT,
            transcendentals=pairs * TILE * TILE * HEADS,
        ),
    )(*operands)


def stack_kernel(count, *refs):
    arrays, (out, done) = refs[:count], refs[count:]
    copies = []
    low = 0
    for n, ref in enumerate(arrays):
        copies.append(pltpu.make_async_copy(ref, out.at[pl.ds(low, ref.shape[0])], done.at[n]))
        copies[-1].start()
        low += ref.shape[0]
    for copy in copies:
        copy.wait()


def stacked(*arrays):
    rows = sum(a.shape[0] for a in arrays)
    anywhere = pl.BlockSpec(memory_space=pltpu.HBM if arrays[0].shape[0] == TILE else pl.ANY)
    return pl.pallas_call(
        functools.partial(stack_kernel, len(arrays)),
        out_shape=jax.ShapeDtypeStruct((rows, arrays[0].shape[1]), arrays[0].dtype),
        in_specs=[anywhere] * len(arrays),
        out_specs=pl.BlockSpec(memory_space=pl.ANY),
        scratch_shapes=[pltpu.SemaphoreType.DMA((len(arrays),))],
        compiler_params=pltpu.CompilerParams(vmem_limit_bytes=2**20),
        cost_estimate=pl.CostEstimate(flops=0, bytes_accessed=4 * rows * FEAT, transcendentals=0),
    )(*arrays)


def merge_kernel(o0, s0, op, om, out):
    own = s0[...]
    peaks, totals, sums = [own], [pltpu.roll(own, HD - 8, 1)], [o0]
    for ref in (op, om):
        stats = ref[:, FEAT:].astype(jnp.float32)
        total = pltpu.roll(stats, HD - 8, 1) + pltpu.roll(stats, HD - 16, 1)
        peaks.append(jnp.where(total > 0, stats, -1e30))
        totals.append(total)
        sums.append(ref)
    peak = jnp.maximum(jnp.maximum(peaks[0], peaks[1]), peaks[2])
    factors = [jnp.exp2(p - peak) for p in peaks]
    total = sum(f * t for f, t in zip(factors, totals))
    shares = [f / total for f in factors]
    for h in range(HEADS):
        cols = slice(h * HD, (h + 1) * HD)
        parts = [w[:, h : h + 1] * ref[:, cols].astype(jnp.float32) for w, ref in zip(shares, sums)]
        out[:, cols] = (parts[0] + parts[1] + parts[2]).astype(jnp.bfloat16)


def merge(*operands):
    return pl.pallas_call(
        merge_kernel,
        out_shape=jax.ShapeDtypeStruct((TILE, FEAT), jnp.bfloat16),
        in_specs=[VMEM] * len(operands),
        out_specs=VMEM,
        compiler_params=pltpu.CompilerParams(vmem_limit_bytes=12 * 1024 * 1024),
        cost_estimate=pl.CostEstimate(flops=10 * TILE * FEAT, bytes_accessed=2**20, transcendentals=0),
    )(*operands)


def project_kernel(_, rows, weight, out):
    product = lax.dot_general(
        rows[...], weight[...], (((1,), (1,)), ((), ())), preferred_element_type=jnp.float32
    )
    out[...] = product.astype(out.dtype)


def project(rows, weight, which, dtype):
    half = weight.shape[0] // 2
    return pl.pallas_call(
        project_kernel,
        grid_spec=pltpu.PrefetchScalarGridSpec(
            num_scalar_prefetch=1,
            grid=(1,),
            in_specs=[
                pl.BlockSpec(rows.shape, lambda i, c: (0, 0)),
                pl.BlockSpec((half, FEAT), lambda i, c: (c[0], 0)),
            ],
            out_specs=pl.BlockSpec((rows.shape[0], half), lambda i, c: (0, 0)),
        ),
        out_shape=jax.ShapeDtypeStruct((rows.shape[0], half), dtype),
        compiler_params=pltpu.CompilerParams(vmem_limit_bytes=56 * 2**20),
        cost_estimate=pl.CostEstimate(
            flops=2 * rows.shape[0] * half * FEAT, bytes_accessed=3 * 2**20, transcendentals=0
        ),
    )(which[None], rows, weight)


PAD = 16
SHARE = 12
WIDE = 8 * 4 * SHARE


def column_order():
    order = np.zeros((4, 8, PAD, WIDE), np.float32)
    for x in range(4):
        for p in range(8):
            for j in range(SHARE):
                order[x, p, j, (p * 4 + x) * SHARE + j] = 1
    return order.reshape(4 * HD, WIDE)


def arrange_kernel(pieces, order, out):
    for z in range(4):
        block = jnp.concatenate([pieces[x, :, z * HD : (z + 1) * HD] for x in range(4)], axis=1)
        product = jnp.dot(block, order[...], preferred_element_type=jnp.float32)
        out[:, z * WIDE : (z + 1) * WIDE] = product.astype(jnp.bfloat16)


def arrange(pieces):
    return pl.pallas_call(
        arrange_kernel,
        out_shape=jax.ShapeDtypeStruct((TILE, 4 * WIDE), jnp.bfloat16),
        in_specs=[VMEM, VMEM],
        out_specs=VMEM,
        compiler_params=pltpu.CompilerParams(vmem_limit_bytes=12 * 1024 * 1024),
        cost_estimate=pl.CostEstimate(flops=2 * TILE * 4 * HD * 4 * WIDE, bytes_accessed=2**20, transcendentals=0),
    )(pieces, jnp.asarray(column_order(), jnp.bfloat16))


def body(queries, keys, values, window, out_weight):
    my_tile = lax.axis_index(TOK)
    core = lax.axis_index("head")
    kv = stacked(keys, values)
    ap = lax.ppermute(kv, ALL, first_axis(1))
    am = lax.ppermute(kv, ALL, first_axis(-1))
    line_y = lax.all_to_all(jnp.broadcast_to(out_weight.T, (8, SHARE, FEAT)), "y", 0, 0)
    bias = biases(window, my_tile, core)
    q0 = with_biases(queries, bias[0])
    qp = lax.ppermute(with_biases(queries, bias[2]), ALL, row_axis(1))
    qm = lax.ppermute(with_biases(queries, bias[1]), ALL, row_axis(-1))
    line = stacked(kv, ap, am)
    line_y, _ = lax.optimization_barrier((line_y, line))
    line_y = jnp.pad(line_y, ((0, 0), (0, PAD - SHARE), (0, 0)))
    weight = lax.all_gather(line_y.reshape(-1, FEAT), "z", tiled=True)
    bp = lax.ppermute(line, ALL, second_axis(1))
    bm = lax.ppermute(line, ALL, second_axis(-1))
    near = [(n, 0, 3 * n) for n in range(3)]
    far = [(n, 2 * TILE * a, 3 * a + n + 1) for n in range(2) for a in range(3)]
    *far_state, own_sum, own_stats = attention((qp, qm, q0), (kv, ap, am), near, parts=(2, 1))
    op, om = attention((qp, qm), (bp, bm), far, far_state, message=True)
    back_p = lax.ppermute(om, ALL, row_axis(1))
    back_m = lax.ppermute(op, ALL, row_axis(-1))
    o0, s0 = attention((q0,), (bp, bm), far, (own_sum, own_stats))
    attended = merge(o0, s0, back_p, back_m)
    rows = lax.all_gather(attended, "x", tiled=True)
    other = project(rows, weight, 1 - core, jnp.bfloat16)
    received = lax.ppermute(other, "head", [(0, 1), (1, 0)])
    mine = project(rows, weight, core, jnp.float32)
    columns = (mine + received.astype(jnp.float32)).astype(jnp.bfloat16)
    pieces = lax.all_to_all(columns.reshape(4, TILE, -1), "x", 0, 0)
    return arrange(pieces)


def solution(mesh):
    fine = Mesh(mesh.devices.reshape(8, 8, 4, 2), ALL)
    in_specs = (P(TOK, "head"), P(TOK, "head"), P(TOK, "head"), P(TOK, None), P("head", TOK))
    return jax.shard_map(body, mesh=fine, in_specs=in_specs, out_specs=P(TOK, "head"), check_vma=False)
```

```python
import functools

import jax
import jax.numpy as jnp
import numpy as np
from jax import lax
from jax.experimental import pallas as pl
from jax.experimental.pallas import tpu as pltpu
from jax.sharding import Mesh, PartitionSpec as P

HD = 128
TILE = 128
HEADS = 6
FEAT = HEADS * HD
TF, TH, TW = 8, 4, 8
TILES = TF * TH * TW
ALL = ("z", "y", "x", "head")
TOK = ("z", "y", "x")
FACTOR = float(HD**-0.5 * np.log2(np.e))
OFFSETS = (0, 1, -1)
FLAG_ROWS = 16


def place(tile):
    return tile // (TH * TW), tile // TW % TH, tile % TW


def from_neighbour(offset_of_core):
    pairs = []
    for tile in range(TILES):
        for core in range(2):
            f, r, c = (a + b for a, b in zip(place(tile), offset_of_core(core)))
            if 0 <= f < TF and 0 <= r < TH and 0 <= c < TW:
                source = (f * TH + r) * TW + c
                pairs.append((2 * source + core, 2 * tile + core))
    return pairs


def first_axis(step):
    return from_neighbour(lambda core: (step, 0, 0) if core == 0 else (0, 0, step))


def second_axis(step):
    return from_neighbour(lambda core: (0, 0, step) if core == 0 else (step, 0, 0))


def row_axis(step):
    return from_neighbour(lambda core: (0, step, 0))


def biases(window, my_tile, core):
    slot = jnp.arange(27, dtype=jnp.int32)

    def step(digit):
        return jnp.where(digit == 2, -1, digit)

    dr, da, db = step(slot // 9), step(slot // 3 % 3), step(slot % 3)
    df = jnp.where(core == 0, da, db)
    dc = jnp.where(core == 0, db, da)
    f, r, c = place(my_tile)
    inside = (
        (f + df >= 0) & (f + df < TF) & (r + dr >= 0) & (r + dr < TH) & (c + dc >= 0) & (c + dc < TW)
    )
    tile = my_tile + (df * TH + dr) * TW + dc
    listed = inside & jnp.any(window[0][None, :] == tile[:, None], axis=1)
    return jnp.where(listed, 0.0, -1e30).astype(jnp.bfloat16).reshape(3, 9)


def with_biases(queries, bias):
    rows = jnp.zeros((FLAG_ROWS,), jnp.bfloat16).at[:9].set(bias)
    return jnp.concatenate([queries, jnp.broadcast_to(rows[:, None], (FLAG_ROWS, queries.shape[1]))])


def attention_kernel(groups, query_count, with_state, message, *refs):
    refs = list(refs)
    q_refs = [refs.pop(0) for _ in range(query_count)]
    kv_refs = [refs.pop(0) for _ in range(max(g[0] for g in groups) + 1)]
    old_sum, old_stats = (refs.pop(0), refs.pop(0)) if with_state else (None, None)
    rows = query_count * TILE
    bias = []
    for ref in q_refs:
        block = ref[TILE : TILE + FLAG_ROWS, :HD].astype(jnp.float32)
        bias.append([block[j : j + 1, :] for _, _, j in groups])
    lane = lax.broadcasted_iota(jnp.int32, (rows, HD), 1)
    stats = jnp.zeros((rows, HD), jnp.float32)
    for h in range(HEADS):
        cols = slice(h * HD, (h + 1) * HD)
        q = jnp.concatenate([ref[:TILE, cols] for ref in q_refs], axis=0)
        k = jnp.concatenate([kv_refs[n][lo : lo + TILE, cols] for n, lo, _ in groups], axis=0)
        v = jnp.concatenate([kv_refs[n][lo + TILE : lo + 2 * TILE, cols] for n, lo, _ in groups], axis=0)
        scores = lax.dot_general(q, k, (((1,), (1,)), ((), ())), preferred_element_type=jnp.float32)
        shifted = jnp.concatenate(
            [
                jnp.concatenate(
                    [
                        scores[i * TILE : (i + 1) * TILE, j * TILE : (j + 1) * TILE] * FACTOR + bias[i][j]
                        for j in range(len(groups))
                    ],
                    axis=1,
                )
                for i in range(query_count)
            ],
            axis=0,
        )
        peak = jnp.max(shifted, axis=1, keepdims=True)
        if with_state:
            old_peak = old_stats[:, h : h + 1]
            peak = jnp.maximum(peak, old_peak)
        peak = peak.astype(jnp.bfloat16).astype(jnp.float32)
        unrounded = jnp.exp2(shifted - peak)
        total = jnp.sum(unrounded, axis=1, keepdims=True)
        summed = jnp.dot(unrounded.astype(jnp.bfloat16), v, preferred_element_type=jnp.float32)
        if with_state:
            factor = jnp.exp2(old_peak - peak)
            total = total + factor * old_stats[:, h + 8 : h + 9]
            summed = summed + factor * old_sum[:, cols]
        stats = jnp.where(lane == h, peak, stats)
        if message:
            high = total.astype(jnp.bfloat16).astype(jnp.float32)
            stats = jnp.where(lane == h + 8, high, stats)
            stats = jnp.where(lane == h + 16, total - high, stats)
            for i in range(query_count):
                refs[i][:, cols] = summed[i * TILE : (i + 1) * TILE].astype(jnp.bfloat16)
        else:
            stats = jnp.where(lane == h + 8, total, stats)
            refs[0][:, cols] = summed
    if message:
        for i in range(query_count):
            refs[i][:, FEAT:] = stats[i * TILE : (i + 1) * TILE].astype(jnp.bfloat16)
    else:
        refs[1][...] = stats


VMEM = pl.BlockSpec(memory_space=pltpu.VMEM)


def attention(queries, pieces, groups, state=None, message=False):
    count = len(queries)
    rows = count * TILE
    if message:
        out_shape = (jax.ShapeDtypeStruct((TILE, FEAT + HD), jnp.bfloat16),) * count
    else:
        out_shape = (
            jax.ShapeDtypeStruct((rows, FEAT), jnp.float32),
            jax.ShapeDtypeStruct((rows, HD), jnp.float32),
        )
    in_specs = [VMEM] * (count + len(pieces))
    operands = [*queries, *pieces]
    if state is not None:
        (total_rows, which), arrays = state
        for array in arrays:
            in_specs.append(pl.BlockSpec((rows, array.shape[1]), lambda i: (which, 0)))
            operands.append(array)
    pairs = count * len(groups)
    return pl.pallas_call(
        functools.partial(attention_kernel, groups, count, state is not None, message),
        grid=(1,),
        out_shape=out_shape,
        in_specs=in_specs,
        out_specs=(VMEM,) * len(out_shape),
        compiler_params=pltpu.CompilerParams(vmem_limit_bytes=12 * 1024 * 1024),
        cost_estimate=pl.CostEstimate(
            flops=60 * pairs * TILE * TILE * FEAT,
            bytes_accessed=len(groups) * 4 * TILE * FEAT,
            transcendentals=pairs * TILE * TILE * HEADS,
        ),
    )(*operands)


def stack_kernel(*refs):
    low = 0
    for ref in refs[:-1]:
        refs[-1][low : low + ref.shape[0], :] = ref[...]
        low += ref.shape[0]


def stacked(*arrays):
    rows = sum(a.shape[0] for a in arrays)
    return pl.pallas_call(
        stack_kernel,
        out_shape=jax.ShapeDtypeStruct((rows, arrays[0].shape[1]), arrays[0].dtype),
        in_specs=[VMEM] * len(arrays),
        out_specs=VMEM,
        compiler_params=pltpu.CompilerParams(vmem_limit_bytes=12 * 1024 * 1024),
        cost_estimate=pl.CostEstimate(flops=0, bytes_accessed=4 * rows * FEAT, transcendentals=0),
    )(*arrays)


def merge_kernel(o0, s0, op, om, out):
    own = s0[...]
    peaks, totals, sums = [own], [pltpu.roll(own, HD - 8, 1)], [o0]
    for ref in (op, om):
        stats = ref[:, FEAT:].astype(jnp.float32)
        total = pltpu.roll(stats, HD - 8, 1) + pltpu.roll(stats, HD - 16, 1)
        peaks.append(jnp.where(total > 0, stats, -1e30))
        totals.append(total)
        sums.append(ref)
    peak = jnp.maximum(jnp.maximum(peaks[0], peaks[1]), peaks[2])
    factors = [jnp.exp2(p - peak) for p in peaks]
    total = sum(f * t for f, t in zip(factors, totals))
    shares = [f / total for f in factors]
    for h in range(HEADS):
        cols = slice(h * HD, (h + 1) * HD)
        parts = [w[:, h : h + 1] * ref[:, cols].astype(jnp.float32) for w, ref in zip(shares, sums)]
        out[:, cols] = (parts[0] + parts[1] + parts[2]).astype(jnp.bfloat16)


def merge(*operands):
    return pl.pallas_call(
        merge_kernel,
        out_shape=jax.ShapeDtypeStruct((TILE, FEAT), jnp.bfloat16),
        in_specs=[VMEM] * len(operands),
        out_specs=VMEM,
        compiler_params=pltpu.CompilerParams(vmem_limit_bytes=12 * 1024 * 1024),
        cost_estimate=pl.CostEstimate(flops=10 * TILE * FEAT, bytes_accessed=2**20, transcendentals=0),
    )(*operands)


def project_kernel(_, rows, weight, out):
    product = lax.dot_general(
        rows[...], weight[...], (((1,), (1,)), ((), ())), preferred_element_type=jnp.float32
    )
    out[...] = product.astype(out.dtype)


def project(rows, weight, which, dtype):
    half = weight.shape[0] // 2
    return pl.pallas_call(
        project_kernel,
        grid_spec=pltpu.PrefetchScalarGridSpec(
            num_scalar_prefetch=1,
            grid=(1,),
            in_specs=[
                pl.BlockSpec(rows.shape, lambda i, c: (0, 0)),
                pl.BlockSpec((half, FEAT), lambda i, c: (c[0], 0)),
            ],
            out_specs=pl.BlockSpec((rows.shape[0], half), lambda i, c: (0, 0)),
        ),
        out_shape=jax.ShapeDtypeStruct((rows.shape[0], half), dtype),
        compiler_params=pltpu.CompilerParams(vmem_limit_bytes=12 * 1024 * 1024),
        cost_estimate=pl.CostEstimate(
            flops=2 * rows.shape[0] * half * FEAT, bytes_accessed=3 * 2**20, transcendentals=0
        ),
    )(which[None], rows, weight)


PAD = 16
SHARE = 12
WIDE = 8 * 4 * SHARE


def column_order():
    order = np.zeros((4, 8, PAD, WIDE), np.float32)
    for x in range(4):
        for p in range(8):
            for j in range(SHARE):
                order[x, p, j, (p * 4 + x) * SHARE + j] = 1
    return order.reshape(4 * HD, WIDE)


def arrange_kernel(pieces, order, out):
    for z in range(4):
        block = jnp.concatenate([pieces[x, :, z * HD : (z + 1) * HD] for x in range(4)], axis=1)
        product = jnp.dot(block, order[...], preferred_element_type=jnp.float32)
        out[:, z * WIDE : (z + 1) * WIDE] = product.astype(jnp.bfloat16)


def arrange(pieces):
    return pl.pallas_call(
        arrange_kernel,
        out_shape=jax.ShapeDtypeStruct((TILE, 4 * WIDE), jnp.bfloat16),
        in_specs=[VMEM, VMEM],
        out_specs=VMEM,
        compiler_params=pltpu.CompilerParams(vmem_limit_bytes=12 * 1024 * 1024),
        cost_estimate=pl.CostEstimate(flops=2 * TILE * 4 * HD * 4 * WIDE, bytes_accessed=2**20, transcendentals=0),
    )(pieces, jnp.asarray(column_order(), jnp.bfloat16))


def body(queries, keys, values, window, out_weight):
    my_tile = lax.axis_index(TOK)
    core = lax.axis_index("head")
    kv = lax.optimization_barrier(jnp.concatenate([keys, values]))
    ap = lax.ppermute(kv, ALL, first_axis(1))
    am = lax.ppermute(kv, ALL, first_axis(-1))
    line_y = lax.all_to_all(jnp.broadcast_to(out_weight.T, (8, SHARE, FEAT)), "y", 0, 0)
    bias = biases(window, my_tile, core)
    q0 = with_biases(queries, bias[0])
    qp = lax.ppermute(with_biases(queries, bias[2]), ALL, row_axis(1))
    qm = lax.ppermute(with_biases(queries, bias[1]), ALL, row_axis(-1))
    line = stacked(kv, ap, am)
    line_y, _ = lax.optimization_barrier((line_y, line))
    line_y = jnp.pad(line_y, ((0, 0), (0, PAD - SHARE), (0, 0)))
    weight = lax.all_gather(line_y.reshape(-1, FEAT), "z", tiled=True)
    bp = lax.ppermute(line, ALL, second_axis(1))
    bm = lax.ppermute(line, ALL, second_axis(-1))
    near = [(n, 0, 3 * n) for n in range(3)]
    far = [(n, 2 * TILE * a, 3 * a + n + 1) for n in range(2) for a in range(3)]
    state = attention((qp, qm, q0), (kv, ap, am), near)
    op, om = attention((qp, qm), (bp, bm), far, ((3, 0), state), message=True)
    back_p = lax.ppermute(om, ALL, row_axis(1))
    back_m = lax.ppermute(op, ALL, row_axis(-1))
    o0, s0 = attention((q0,), (bp, bm), far, ((3, 2), state))
    attended = merge(o0, s0, back_p, back_m)
    rows = lax.all_gather(attended, "x", tiled=True)
    other = project(rows, weight, 1 - core, jnp.bfloat16)
    received = lax.ppermute(other, "head", [(0, 1), (1, 0)])
    mine = project(rows, weight, core, jnp.float32)
    columns = (mine + received.astype(jnp.float32)).astype(jnp.bfloat16)
    pieces = lax.all_to_all(columns.reshape(4, TILE, -1), "x", 0, 0)
    return arrange(pieces)


def solution(mesh):
    fine = Mesh(mesh.devices.reshape(8, 8, 4, 2), ALL)
    in_specs = (P(TOK, "head"), P(TOK, "head"), P(TOK, "head"), P(TOK, None), P("head", TOK))
    return jax.shard_map(body, mesh=fine, in_specs=in_specs, out_specs=P(TOK, "head"), check_vma=False)
```

```python
import functools

import jax
import jax.numpy as jnp
import numpy as np
from jax import lax
from jax.experimental import pallas as pl
from jax.experimental.pallas import tpu as pltpu
from jax.sharding import Mesh, PartitionSpec as P

HD = 128
TILE = 128
HEADS = 6
FEAT = HEADS * HD
TF, TH, TW = 8, 4, 8
TILES = TF * TH * TW
ALL = ("z", "y", "x", "head")
TOK = ("z", "y", "x")
FACTOR = float(HD**-0.5 * np.log2(np.e))
OFFSETS = (0, 1, -1)
FLAG_ROWS = 16


def place(tile):
    return tile // (TH * TW), tile // TW % TH, tile % TW


def from_neighbour(offset_of_core):
    pairs = []
    for tile in range(TILES):
        for core in range(2):
            f, r, c = (a + b for a, b in zip(place(tile), offset_of_core(core)))
            if 0 <= f < TF and 0 <= r < TH and 0 <= c < TW:
                source = (f * TH + r) * TW + c
                pairs.append((2 * source + core, 2 * tile + core))
    return pairs


def first_axis(step):
    return from_neighbour(lambda core: (step, 0, 0) if core == 0 else (0, 0, step))


def second_axis(step):
    return from_neighbour(lambda core: (0, 0, step) if core == 0 else (step, 0, 0))


def row_axis(step):
    return from_neighbour(lambda core: (0, step, 0))


def biases(window, my_tile, core):
    slot = jnp.arange(27, dtype=jnp.int32)

    def step(digit):
        return jnp.where(digit == 2, -1, digit)

    dr, da, db = step(slot // 9), step(slot // 3 % 3), step(slot % 3)
    df = jnp.where(core == 0, da, db)
    dc = jnp.where(core == 0, db, da)
    f, r, c = place(my_tile)
    inside = (
        (f + df >= 0) & (f + df < TF) & (r + dr >= 0) & (r + dr < TH) & (c + dc >= 0) & (c + dc < TW)
    )
    tile = my_tile + (df * TH + dr) * TW + dc
    listed = inside & jnp.any(window[0][None, :] == tile[:, None], axis=1)
    return jnp.where(listed, 0.0, -1e30).astype(jnp.bfloat16).reshape(3, 9)


def with_biases(queries, bias):
    rows = jnp.zeros((FLAG_ROWS,), jnp.bfloat16).at[:9].set(bias)
    return jnp.concatenate([queries, jnp.broadcast_to(rows[:, None], (FLAG_ROWS, queries.shape[1]))])


def attention_kernel(groups, query_count, with_state, message, *refs):
    refs = list(refs)
    q_refs = [refs.pop(0) for _ in range(query_count)]
    kv_refs = [refs.pop(0) for _ in range(max(g[0] for g in groups) + 1)]
    old_sum, old_stats = (refs.pop(0), refs.pop(0)) if with_state else (None, None)
    rows = query_count * TILE
    bias = []
    for ref in q_refs:
        block = ref[TILE : TILE + FLAG_ROWS, :HD].astype(jnp.float32)
        bias.append([block[j : j + 1, :] for _, _, j in groups])
    lane = lax.broadcasted_iota(jnp.int32, (rows, HD), 1)
    stats = jnp.zeros((rows, HD), jnp.float32)
    for h in range(HEADS):
        cols = slice(h * HD, (h + 1) * HD)
        q = jnp.concatenate([ref[:TILE, cols] for ref in q_refs], axis=0)
        k = jnp.concatenate([kv_refs[n][lo : lo + TILE, cols] for n, lo, _ in groups], axis=0)
        v = jnp.concatenate([kv_refs[n][lo + TILE : lo + 2 * TILE, cols] for n, lo, _ in groups], axis=0)
        scores = lax.dot_general(q, k, (((1,), (1,)), ((), ())), preferred_element_type=jnp.float32)
        shifted = jnp.concatenate(
            [
                jnp.concatenate(
                    [
                        scores[i * TILE : (i + 1) * TILE, j * TILE : (j + 1) * TILE] * FACTOR + bias[i][j]
                        for j in range(len(groups))
                    ],
                    axis=1,
                )
                for i in range(query_count)
            ],
            axis=0,
        )
        peak = jnp.max(shifted, axis=1, keepdims=True)
        if with_state:
            old_peak = old_stats[:, h : h + 1]
            peak = jnp.maximum(peak, old_peak)
        peak = peak.astype(jnp.bfloat16).astype(jnp.float32)
        unrounded = jnp.exp2(shifted - peak)
        total = jnp.sum(unrounded, axis=1, keepdims=True)
        summed = jnp.dot(unrounded.astype(jnp.bfloat16), v, preferred_element_type=jnp.float32)
        if with_state:
            factor = jnp.exp2(old_peak - peak)
            total = total + factor * old_stats[:, h + 8 : h + 9]
            summed = summed + factor * old_sum[:, cols]
        stats = jnp.where(lane == h, peak, stats)
        if message:
            high = total.astype(jnp.bfloat16).astype(jnp.float32)
            stats = jnp.where(lane == h + 8, high, stats)
            stats = jnp.where(lane == h + 16, total - high, stats)
            for i in range(query_count):
                refs[i][:, cols] = summed[i * TILE : (i + 1) * TILE].astype(jnp.bfloat16)
        else:
            stats = jnp.where(lane == h + 8, total, stats)
            refs[0][:, cols] = summed
    if message:
        for i in range(query_count):
            refs[i][:, FEAT:] = stats[i * TILE : (i + 1) * TILE].astype(jnp.bfloat16)
    else:
        refs[1][...] = stats


VMEM = pl.BlockSpec(memory_space=pltpu.VMEM)


def attention(queries, pieces, groups, state=None, message=False):
    count = len(queries)
    rows = count * TILE
    if message:
        out_shape = (jax.ShapeDtypeStruct((TILE, FEAT + HD), jnp.bfloat16),) * count
    else:
        out_shape = (
            jax.ShapeDtypeStruct((rows, FEAT), jnp.float32),
            jax.ShapeDtypeStruct((rows, HD), jnp.float32),
        )
    in_specs = [VMEM] * (count + len(pieces))
    operands = [*queries, *pieces]
    if state is not None:
        (total_rows, which), arrays = state
        for array in arrays:
            in_specs.append(pl.BlockSpec((rows, array.shape[1]), lambda i: (which, 0)))
            operands.append(array)
    pairs = count * len(groups)
    return pl.pallas_call(
        functools.partial(attention_kernel, groups, count, state is not None, message),
        grid=(1,),
        out_shape=out_shape,
        in_specs=in_specs,
        out_specs=(VMEM,) * len(out_shape),
        compiler_params=pltpu.CompilerParams(vmem_limit_bytes=12 * 1024 * 1024),
        cost_estimate=pl.CostEstimate(
            flops=60 * pairs * TILE * TILE * FEAT,
            bytes_accessed=len(groups) * 4 * TILE * FEAT,
            transcendentals=pairs * TILE * TILE * HEADS,
        ),
    )(*operands)


def stack_kernel(*refs):
    low = 0
    for ref in refs[:-1]:
        refs[-1][low : low + ref.shape[0], :] = ref[...]
        low += ref.shape[0]


def stacked(*arrays):
    rows = sum(a.shape[0] for a in arrays)
    return pl.pallas_call(
        stack_kernel,
        out_shape=jax.ShapeDtypeStruct((rows, arrays[0].shape[1]), arrays[0].dtype),
        in_specs=[VMEM] * len(arrays),
        out_specs=VMEM,
        compiler_params=pltpu.CompilerParams(vmem_limit_bytes=12 * 1024 * 1024),
        cost_estimate=pl.CostEstimate(flops=0, bytes_accessed=4 * rows * FEAT, transcendentals=0),
    )(*arrays)


def merge_kernel(o0, s0, op, om, out):
    own = s0[...]
    peaks, totals, sums = [own], [pltpu.roll(own, HD - 8, 1)], [o0]
    for ref in (op, om):
        stats = ref[:, FEAT:].astype(jnp.float32)
        total = pltpu.roll(stats, HD - 8, 1) + pltpu.roll(stats, HD - 16, 1)
        peaks.append(jnp.where(total > 0, stats, -1e30))
        totals.append(total)
        sums.append(ref)
    peak = jnp.maximum(jnp.maximum(peaks[0], peaks[1]), peaks[2])
    factors = [jnp.exp2(p - peak) for p in peaks]
    total = sum(f * t for f, t in zip(factors, totals))
    shares = [f / total for f in factors]
    for h in range(HEADS):
        cols = slice(h * HD, (h + 1) * HD)
        parts = [w[:, h : h + 1] * ref[:, cols].astype(jnp.float32) for w, ref in zip(shares, sums)]
        out[:, cols] = (parts[0] + parts[1] + parts[2]).astype(jnp.bfloat16)


def merge(*operands):
    return pl.pallas_call(
        merge_kernel,
        out_shape=jax.ShapeDtypeStruct((TILE, FEAT), jnp.bfloat16),
        in_specs=[VMEM] * len(operands),
        out_specs=VMEM,
        compiler_params=pltpu.CompilerParams(vmem_limit_bytes=12 * 1024 * 1024),
        cost_estimate=pl.CostEstimate(flops=10 * TILE * FEAT, bytes_accessed=2**20, transcendentals=0),
    )(*operands)


def project_kernel(rows, weight, out):
    product = lax.dot_general(
        rows[...], weight[...], (((1,), (1,)), ((), ())), preferred_element_type=jnp.float32
    )
    out[...] = product.astype(out.dtype)


def project(rows, weight, which, dtype):
    half = weight.shape[0] // 2
    part = lax.dynamic_slice_in_dim(weight, which * half, half, 0)
    return pl.pallas_call(
        project_kernel,
        out_shape=jax.ShapeDtypeStruct((rows.shape[0], half), dtype),
        in_specs=[VMEM, VMEM],
        out_specs=VMEM,
        compiler_params=pltpu.CompilerParams(vmem_limit_bytes=12 * 1024 * 1024),
        cost_estimate=pl.CostEstimate(
            flops=2 * rows.shape[0] * half * FEAT, bytes_accessed=3 * 2**20, transcendentals=0
        ),
    )(rows, part)


PAD = 16
SHARE = 12
WIDE = 8 * 4 * SHARE


def column_order():
    order = np.zeros((4, 8, PAD, WIDE), np.float32)
    for x in range(4):
        for p in range(8):
            for j in range(SHARE):
                order[x, p, j, (p * 4 + x) * SHARE + j] = 1
    return order.reshape(4 * HD, WIDE)


def arrange_kernel(pieces, order, out):
    for z in range(4):
        block = jnp.concatenate([pieces[x, :, z * HD : (z + 1) * HD] for x in range(4)], axis=1)
        product = jnp.dot(block, order[...], preferred_element_type=jnp.float32)
        out[:, z * WIDE : (z + 1) * WIDE] = product.astype(jnp.bfloat16)


def arrange(pieces):
    return pl.pallas_call(
        arrange_kernel,
        out_shape=jax.ShapeDtypeStruct((TILE, 4 * WIDE), jnp.bfloat16),
        in_specs=[VMEM, VMEM],
        out_specs=VMEM,
        compiler_params=pltpu.CompilerParams(vmem_limit_bytes=12 * 1024 * 1024),
        cost_estimate=pl.CostEstimate(flops=2 * TILE * 4 * HD * 4 * WIDE, bytes_accessed=2**20, transcendentals=0),
    )(pieces, jnp.asarray(column_order(), jnp.bfloat16))


def body(queries, keys, values, window, out_weight):
    my_tile = lax.axis_index(TOK)
    core = lax.axis_index("head")
    kv = lax.optimization_barrier(jnp.concatenate([keys, values]))
    ap = lax.ppermute(kv, ALL, first_axis(1))
    am = lax.ppermute(kv, ALL, first_axis(-1))
    line_y = lax.all_to_all(jnp.broadcast_to(out_weight.T, (8, SHARE, FEAT)), "y", 0, 0)
    bias = biases(window, my_tile, core)
    q0 = with_biases(queries, bias[0])
    qp = lax.ppermute(with_biases(queries, bias[2]), ALL, row_axis(1))
    qm = lax.ppermute(with_biases(queries, bias[1]), ALL, row_axis(-1))
    line = stacked(kv, ap, am)
    line_y, _ = lax.optimization_barrier((line_y, line))
    line_y = jnp.pad(line_y, ((0, 0), (0, PAD - SHARE), (0, 0)))
    weight = lax.all_gather(line_y.reshape(-1, FEAT), "z", tiled=True)
    bp = lax.ppermute(line, ALL, second_axis(1))
    bm = lax.ppermute(line, ALL, second_axis(-1))
    near = [(n, 0, 3 * n) for n in range(3)]
    far = [(n, 2 * TILE * a, 3 * a + n + 1) for n in range(2) for a in range(3)]
    state = attention((qp, qm, q0), (kv, ap, am), near)
    op, om = attention((qp, qm), (bp, bm), far, ((3, 0), state), message=True)
    back_p = lax.ppermute(om, ALL, row_axis(1))
    back_m = lax.ppermute(op, ALL, row_axis(-1))
    o0, s0 = attention((q0,), (bp, bm), far, ((3, 2), state))
    attended = merge(o0, s0, back_p, back_m)
    rows = lax.all_gather(attended, "x", tiled=True)
    other = project(rows, weight, 1 - core, jnp.bfloat16)
    received = lax.ppermute(other, "head", [(0, 1), (1, 0)])
    weight, _ = lax.optimization_barrier((weight, other))
    mine = project(rows, weight, core, jnp.float32)
    columns = (mine + received.astype(jnp.float32)).astype(jnp.bfloat16)
    pieces = lax.all_to_all(columns.reshape(4, TILE, -1), "x", 0, 0)
    return arrange(pieces)


def solution(mesh):
    fine = Mesh(mesh.devices.reshape(8, 8, 4, 2), ALL)
    in_specs = (P(TOK, "head"), P(TOK, "head"), P(TOK, "head"), P(TOK, None), P("head", TOK))
    return jax.shard_map(body, mesh=fine, in_specs=in_specs, out_specs=P(TOK, "head"), check_vma=False)
```
